256 devices in a mesh: seq: 32 (over x, z_hi, core), vocab: 8 (over z_lo, y).
Axes of the slice: x: 4, y: 4, z: 8 (z_hi: 4, z_lo: 2; z = z_hi * 2 + z_lo), core: 2. Of those that a mesh axis runs over, the one named last changes fastest.
Arguments:
- rollout_hidden: bfloat16 [1024, 4096], P('seq', 'vocab'), may hold values from -200 to 200
- trainer_hidden: bfloat16 [1024, 4096], P('seq'), may hold values from -200 to 200
- head_weight: bfloat16 [4096, 151552], P(None, ('seq', 'vocab')), may hold values from -1 to 1
- token_ids: int32 [1024], P('seq'), may hold values from 0 to 151551
- response_mask: int32 [1024], P('seq'), may hold values 0 or 1
- trainer_slot: int32 [1024], P('seq'), may hold values from 0 to 1023, as said below
Outputs:
- intersection: float32 [1024], P('seq')
- distance: float32 [1024], P('seq')
- import_weight: float32 [1024], P('seq')
The draws below stay inside these ranges and needn't reach their ends.
Inputs may be any that keep to these rules, and one draw needn't show every extreme that they name: `trainer_slot`: a permutation of the 1024 trainer positions.
All inputs are finite; a program needn't handle non-finite values. No bound on the sum of `response_mask` on one device may be relied on, other than what follows from the above.
Results may differ from the reference program's by a relative error of at most 0.0025.
Values may be sent and summed in bfloat16 or wider, within the bound.
A program may use at most 128 MiB of HBM per device.

```python
import math
import jax
import jax.numpy as jnp
from jax import lax

D = 4096
VOCAB = 151552
TOKENS = 1024


def shared_anchors(key):
    anchor_key = jax.random.fold_in(key, 301)
    return jnp.clip(jax.random.normal(anchor_key, (6, D)), -4.0, 4.0)


def shared_slots(key):
    slot_key = jax.random.fold_in(key, 211)
    return jax.random.permutation(slot_key, TOKENS).astype(jnp.int32)


def shared_rows(key, low_scale, high_scale, anchor_gain):
    value_key = jax.random.fold_in(key, 221)
    scale_key = jax.random.fold_in(key, 222)
    values = 3.0 * jnp.clip(jax.random.normal(value_key, (TOKENS, D)), -4.0, 4.0)
    scales = jnp.exp(jax.random.uniform(scale_key, (TOKENS, 1), minval=math.log(low_scale), maxval=math.log(high_scale)))
    anchors = shared_anchors(key)
    peaks = anchor_gain * jnp.array([120.0, 180.0, 240.0, 120.0, 180.0, 240.0], jnp.float32) / math.sqrt(D)
    anchor_rows = jnp.arange(6, dtype=jnp.int32) * (TOKENS // 6) + 1
    planted = jnp.zeros((TOKENS, D), jnp.float32).at[anchor_rows].set(anchors * peaks[:, None])
    return (values * scales + planted, scales)


def draw_rollout_hidden(key, part):
    values, scales = shared_rows(key, 0.6, 1.7, 0.5)
    return jnp.clip(values, -199.0, 199.0).astype(jnp.bfloat16)


def draw_trainer_hidden(key, part):
    slots = shared_slots(key)
    values, scales = shared_rows(key, 0.6, 1.7, 0.5)
    key = jax.random.fold_in(key, 5)
    noise_key, rate_key = jax.random.split(key)
    rates = jnp.exp(jax.random.uniform(rate_key, (TOKENS, 1), minval=math.log(0.005), maxval=math.log(0.4)))
    noisy = values + 3.0 * rates * scales * jnp.clip(jax.random.normal(noise_key, (TOKENS, D)), -4.0, 4.0)
    placed = jnp.zeros((TOKENS, D), jnp.float32).at[slots].set(noisy)
    return jnp.clip(placed, -199.0, 199.0).astype(jnp.bfloat16)


def draw_head_weight(key, part):
    anchors = shared_anchors(key)
    key = jax.random.fold_in(key, 7)
    value_key, gain_key = jax.random.split(key)
    low_gain, high_gain, lift = (0.6, 1.7, 0.45)
    position = jnp.arange(VOCAB, dtype=jnp.float32) / VOCAB
    rough = jnp.exp(jax.random.uniform(gain_key, (VOCAB,), minval=math.log(low_gain), maxval=math.log(high_gain)))
    gains = (0.8 + lift * position) * rough
    weight = jnp.clip(jax.random.normal(value_key, (D, VOCAB)), -4.5, 4.5) * gains[None, :] / math.sqrt(D)
    anchor_columns = jnp.arange(6, dtype=jnp.int32) * (VOCAB // 6) + 3
    weight = weight.at[:, anchor_columns].set(anchors.T / math.sqrt(D))
    weight = weight.at[:, anchor_columns + 1].set(0.99 * anchors.T / math.sqrt(D))
    return jnp.clip(weight, -1.0, 1.0).astype(jnp.bfloat16)


def draw_trainer_slot(key, part):
    return shared_slots(key)


def set_ends(drawn, key, least, top_value):
    spot = [jax.random.randint(jax.random.fold_in(key, axis), (), 0, length) for axis, length in enumerate(drawn.shape)]
    widest = drawn.shape.index(max(drawn.shape))
    beside = spot[:widest] + [(spot[widest] + 1) % drawn.shape[widest]] + spot[widest + 1:]
    return drawn.at[tuple(spot)].set(least).at[tuple(beside)].set(top_value)


def setup_inputs(seed: int = 0) -> dict:
    arg_keys = jax.random.split(jax.random.key(seed), 7)
    rollout_hidden = draw_rollout_hidden(jax.random.fold_in(arg_keys[6], 71), 0)
    trainer_hidden = draw_trainer_hidden(jax.random.fold_in(arg_keys[6], 71), 0)
    head_weight = draw_head_weight(jax.random.fold_in(arg_keys[6], 71), 0)
    token_ids = set_ends(jax.random.randint(arg_keys[3], (TOKENS,), 0, VOCAB), jax.random.fold_in(arg_keys[3], 1), 0, VOCAB - 1).astype(jnp.int32)
    response_mask = set_ends((jax.random.randint(arg_keys[4], (TOKENS,), 0, 4) < 3).astype(jnp.int32), jax.random.fold_in(arg_keys[4], 1), 0, 1)
    trainer_slot = draw_trainer_slot(jax.random.fold_in(arg_keys[6], 71), 0)
    return dict(rollout_hidden=rollout_hidden, trainer_hidden=trainer_hidden, head_weight=head_weight, token_ids=token_ids, response_mask=response_mask, trainer_slot=trainer_slot)


def one_block(head_weight, pieces):
    roll_rows, train_rows, sampled, live = pieces
    roll_logit = jnp.dot(roll_rows, head_weight, preferred_element_type=jnp.float32)
    train_logit = jnp.dot(train_rows, head_weight, preferred_element_type=jnp.float32)
    top_roll = lax.optimization_barrier(jnp.max(roll_logit, axis=1, keepdims=True))
    top_train = lax.optimization_barrier(jnp.max(train_logit, axis=1, keepdims=True))
    total_roll = lax.optimization_barrier(jnp.sum(jnp.exp(roll_logit - top_roll), axis=1, keepdims=True))
    total_train = lax.optimization_barrier(jnp.sum(jnp.exp(train_logit - top_train), axis=1, keepdims=True))
    roll_prob = jnp.exp(roll_logit - top_roll) / total_roll
    train_prob = jnp.exp(train_logit - top_train) / total_train
    shared = lax.optimization_barrier(jnp.sum(jnp.minimum(roll_prob, train_prob), axis=1))
    squares = lax.optimization_barrier(jnp.sum((train_prob - roll_prob) ** 2, axis=1))
    pick_roll = jnp.take_along_axis(roll_logit, sampled[:, None], axis=1)
    pick_train = jnp.take_along_axis(train_logit, sampled[:, None], axis=1)
    log_ratio = pick_train - top_train - jnp.log(total_train) - (pick_roll - top_roll - jnp.log(total_roll))
    mask_value = live.astype(jnp.float32)
    ratio = jnp.minimum(jnp.exp(log_ratio[:, 0]), 2.0)
    return (shared * mask_value, jnp.sqrt(squares + 1e-06) * mask_value, ratio * mask_value)

def reference(rollout_hidden, trainer_hidden, head_weight, token_ids, response_mask, trainer_slot):
    arranged = jnp.zeros_like(rollout_hidden).at[trainer_slot].set(rollout_hidden)
    block_count = TOKENS // 128
    results = lax.map(lambda pieces: one_block(head_weight, pieces), (arranged.reshape(block_count, 128, D), trainer_hidden.reshape(block_count, 128, D), token_ids.reshape(block_count, 128), response_mask.reshape(block_count, 128)))
    return (results[0].reshape(TOKENS), results[1].reshape(TOKENS), results[2].reshape(TOKENS))
```

```python
import jax
import jax.numpy as jnp
from jax import lax
from jax.experimental import pallas as pl
from jax.experimental.pallas import tpu as pltpu
from jax.sharding import PartitionSpec as P

MESH = pl.DeviceIdType.MESH
BF16 = jnp.bfloat16
F32 = jnp.float32
NX, NY, NZ, NH = 4, 4, 8, 4
ROWS = 32
HALF = 16
D = 4096
FEAT = 512
COLS = 592
TOK = 512
GROUP = 128


def kernel(roll_in, train_in, head_in, meta_in, mask_in, shared_out, dist_out, ratio_out,
           w, t, r, meta, onehot, perm, lt, lr, stat_r, stat_t, a1, a2, fin, out2, a3,
           ssem, in_sem, w_sem, tx, tz, r1z, m1z, r1x, m1x, msw, ry, rz, yr, zlate, sw, a_sem):
    s, v = lax.axis_index("seq"), lax.axis_index("vocab")
    x, zh, c = s // 8, (s // 2) % 4, s % 2
    zl, y = v // 4, v % 4
    z = zh * 2 + zl

    def dev(dx=0, dy=0, dz=0):
        xx, yy, zz = (x + dx + NX) % NX, (y + dy + NY) % NY, (z + dz + NZ) % NZ
        return ((xx * 4 + zz // 2) * 2 + c, (zz % 2) * 4 + yy)

    partner = (s + 1 - 2 * c, v)
    xm, xp, xo = (x + 3) % 4, (x + 1) % 4, (x + 2) % 4
    xg = (x, xm, xp, xo)
    zm, zp, zo = (zh + 3) % 4, (zh + 1) % 4, (zh + 2) % 4

    copies = [
        pltpu.make_async_copy(roll_in, r.at[v, c, x, :, zh], in_sem.at[0]),
        pltpu.make_async_copy(train_in, t.at[x, zh], in_sem.at[1]),
        pltpu.make_async_copy(meta_in, meta.at[c, x, zh], in_sem.at[2]),
        pltpu.make_async_copy(head_in, w.at[0], in_sem.at[3]),
    ]
    for cp in copies:
        cp.start()

    barrier = pltpu.get_barrier_semaphore()
    near = [partner] + [dev(dx=d) for d in (1, -1, 2)] + [dev(dy=d) for d in (1, -1)]
    near += [dev(dz=d) for d in (1, -1, 2, -2, 4)]
    for to in near:
        pl.semaphore_signal(barrier, inc=1, device_id=to, device_id_type=MESH)
    for cp in copies[:3]:
        cp.wait()
    pl.semaphore_wait(barrier, len(near))

    sends = []

    def put(src, dst, rsem, to):
        cp = pltpu.make_async_remote_copy(
            src_ref=src, dst_ref=dst, send_sem=ssem.at[len(sends)], recv_sem=rsem,
            device_id=to, device_id_type=MESH)
        cp.start()
        sends.append(cp)

    def same(ref, rsem, to):
        put(ref, ref, rsem, to)

    def got(ref, rsem):
        pltpu.make_async_remote_copy(
            src_ref=ref, dst_ref=ref, send_sem=rsem, recv_sem=rsem,
            device_id=partner, device_id_type=MESH).wait_recv()

    right, left = dev(dz=1), dev(dz=-1)
    xr, xl = dev(dx=1), dev(dx=-1)
    yu, yd = dev(dy=1), dev(dy=-1)

    own = r.at[v, c, x, :, zh]
    mine = meta.at[c, x, zh]
    for k, d in enumerate((2, -2, 4)):
        same(own, r1z.at[k], dev(dz=d))
    for k, d in enumerate((2, -2, 4)):
        same(mine, m1z.at[k], dev(dz=d))

    outward = dev(dz=2 * zl - 1)

    def ring_begin(g, xx):
        for k in range(2):
            h = zl * k + (1 - zl) * (1 - k)
            same(t.at[xx, zh, h], tz.at[g, 1 - zl, k], outward)

    inward = dev(dz=1 - 2 * zl)
    z_near, z_away = (1 - zl) * zm + zl * zp, (1 - zl) * zp + zl * zm

    def ring_block(xx, side, k):
        if side == 0:
            return t.at[xx, z_near if k < 2 else zo, (zl, 1 - zl, zl)[k]]
        return t.at[xx, z_away if k < 2 else zo, (1 - zl, zl, 1 - zl)[k]]

    def ring_step(g, xx, k, then=None):
        a, b = ring_block(xx, 0, k), ring_block(xx, 1, k)
        got(a, tz.at[g, zl, k])
        same(a, tz.at[g, zl, k], inward)
        if then is not None:
            then(a, 2 + 2 * k)
        got(b, tz.at[g, 1 - zl, k])
        if k == 0:
            same(b, tz.at[g, 1 - zl, 2], outward)
        if then is not None:
            then(b, 3 + 2 * k)

    def to_x(ref, n):
        same(ref, tx.at[0, n], xr)
        same(ref, tx.at[1, n], xl)

    ring_begin(0, x)
    to_x(t.at[x, zh, 0], 0)
    to_x(t.at[x, zh, 1], 1)
    copies[3].wait()
    put(w.at[0], w.at[1], w_sem, partner)

    v_z = (1 - zl) * 4 + y
    v_up, v_dn, v_far = zl * 4 + (y + 1) % 4, zl * 4 + (y + 3) % 4, zl * 4 + (y + 2) % 4
    w_up, w_dn, w_far = (1 - zl) * 4 + (y + 1) % 4, (1 - zl) * 4 + (y + 3) % 4, (1 - zl) * 4 + (y + 2) % 4

    def spread(g):
        block = r.at[v, c, xg[g]]
        same(block, ry.at[0, 0, g], yu)
        same(block, ry.at[1, 0, g], yd)
        same(r.at[v, c, xg[g], 0], rz.at[0, g], right)
        same(r.at[v, c, xg[g], 1], rz.at[1, g], left)

    def swap(n, vv):
        same(r.at[vv, c], sw.at[n], partner)

    def swapped(n, vv):
        got(r.at[vv, 1 - c], sw.at[n])

    for k, zz in enumerate((zm, zp, zo)):
        got(r.at[v, c, x, :, zz], r1z.at[k])
    same(r.at[v, c, x], r1x.at[0, 0], xr)
    same(r.at[v, c, x], r1x.at[1, 0], xl)
    spread(0)
    for k, zz in enumerate((zm, zp, zo)):
        got(meta.at[c, x, zz], m1z.at[k])
    for k, d in enumerate((1, -1, 2)):
        same(meta.at[c, x], m1x.at[k], dev(dx=d))
    got(t.at[xm, zh, 0], tx.at[0, 0])
    same(t.at[xm, zh, 0], tx.at[0, 8], xr)
    got(t.at[xp, zh, 0], tx.at[1, 0])
    got(t.at[xp, zh, 1], tx.at[1, 1])
    same(t.at[xp, zh, 1], tx.at[1, 8], xl)
    got(t.at[xm, zh, 1], tx.at[0, 1])
    ring_step(0, x, 0, to_x)
    got(r.at[v, c, xm], r1x.at[0, 0])
    same(r.at[v, c, xm, 0], r1x.at[0, 1], xr)
    spread(1)
    got(r.at[v, c, xp], r1x.at[1, 0])
    same(r.at[v, c, xp, 1], r1x.at[1, 1], xl)
    spread(2)
    ring_step(0, x, 1, to_x)

    def cross(g):
        got(r.at[v_z, c, xg[g], 0], rz.at[0, g])
        got(r.at[v_z, c, xg[g], 1], rz.at[1, g])
        same(r.at[v_z, c, xg[g]], ry.at[0, 1, g], yu)
        same(r.at[v_z, c, xg[g]], ry.at[1, 1, g], yd)

    def relay(g):
        got(r.at[v_up, c, xg[g]], ry.at[1, 0, g])
        same(r.at[v_up, c, xg[g], 0], yr.at[1, g], yd)
        got(r.at[v_dn, c, xg[g]], ry.at[0, 0, g])
        same(r.at[v_dn, c, xg[g], 1], yr.at[0, g], yu)

    got(r.at[v, c, xo, 0], r1x.at[0, 1])
    got(r.at[v, c, xo, 1], r1x.at[1, 1])
    spread(3)
    swap(0, v)
    for k, xx in enumerate((xm, xp, xo)):
        got(meta.at[c, xx], m1x.at[k])
    same(meta.at[c], msw, partner)
    got(t.at[xo, zh, 0], tx.at[0, 8])
    got(t.at[xo, zh, 1], tx.at[1, 8])
    ring_begin(1, xo)
    cross(0)
    relay(0)
    ring_step(0, x, 2, to_x)
    cross(1)
    cross(2)
    relay(1)
    relay(2)

    got(meta.at[1 - c], msw)
    place = lax.broadcasted_iota(jnp.int32, (TOK, GROUP), 0)
    for cc in range(2):
        for xx in range(NX):
            slot = meta[cc, xx, 0, 0:1, :]
            for zz in range(1, NH):
                slot = slot + meta[cc, xx, zz, 0:1, :]
            token = (slot >> 6) * ROWS + (slot & (ROWS - 1))
            token = jnp.where(((slot >> 5) & 1) == c, token, -1)
            n = cc * NX + xx
            onehot[:, n * GROUP:(n + 1) * GROUP] = jnp.where(place == token, 1.0, 0.0).astype(BF16)

    def rollout_part(vv, first):
        rows = r[vv].reshape(2 * TOK, FEAT)
        perm[...] = jnp.dot(onehot[...], rows, preferred_element_type=F32).astype(BF16)
        for n in range(2):
            part = jnp.dot(perm[...], w[n, pl.ds(pl.multiple_of(vv * FEAT, FEAT), FEAT), :], preferred_element_type=F32)
            if first:
                lr[n] = part
            else:
                lr[n] += part

    def trainer_part(xa, xb):
        def step(k, carry):
            f = pl.ds(pl.multiple_of(k * FEAT, FEAT), FEAT)
            a = t[xa, :, :, :, f].reshape(GROUP, FEAT)
            b = t[xb, :, :, :, f].reshape(GROUP, FEAT)
            rows = jnp.concatenate([a, b], axis=0)
            keep = jnp.where(k == 0, 0.0, 1.0)
            for n in range(2):
                part = jnp.dot(rows, w[n, f, :], preferred_element_type=F32)

                @pl.when(k == 0)
                def _():
                    lt[n, xa] = part[:GROUP]
                    lt[n, xb] = part[GROUP:]

                @pl.when(k > 0)
                def _():
                    lt[n, xa] += part[:GROUP]
                    lt[n, xb] += part[GROUP:]
            return carry
        lax.fori_loop(0, D // FEAT, step, 0)

    lane = lax.broadcasted_iota(jnp.int32, (GROUP, 128), 1)
    column = lax.broadcasted_iota(jnp.int32, (GROUP, COLS), 1)
    offsets = ((s * 8 + v) * COLS, ((s + 1 - 2 * c) * 8 + v) * COLS)
    diagonal = lax.broadcasted_iota(jnp.int32, (GROUP, 128), 0) == lane

    def local_stats(logit, stat, xx, rows):
        ids = meta[c, xx, 0, 1:2, :]
        for zz in range(1, NH):
            ids = ids + meta[c, xx, zz, 1:2, :]
        ids = jnp.sum(jnp.where(diagonal, ids, 0), axis=1, keepdims=True)
        parts = [logit[(n,) + rows] for n in range(2)]
        top = jnp.maximum(jnp.max(parts[0], axis=1, keepdims=True), jnp.max(parts[1], axis=1, keepdims=True))
        total = jnp.zeros((GROUP, 1), F32)
        pick = jnp.zeros((GROUP, 1), F32)
        for n in range(2):
            e = jnp.exp(parts[n] - top)
            logit[(n,) + rows] = e
            total = total + jnp.sum(e, axis=1, keepdims=True)
            pick = pick + jnp.sum(jnp.where(column == ids - offsets[n], parts[n], 0.0), axis=1, keepdims=True)
        table = jnp.where(lane == 0, top, jnp.where(lane == 1, total, jnp.where(lane == 2, pick, 0.0)))
        stat[xx] = jnp.transpose(table)[:8]

    got(w.at[1], w_sem)
    swapped(0, v)
    rollout_part(v, True)

    cross(3)
    relay(3)
    swap(1, v_z)
    swap(2, v_up)
    swap(3, v_dn)
    ring_step(1, xo, 0)

    def far(g):
        got(r.at[v_far, c, xg[g], 0], yr.at[1, g])
        same(r.at[v_far, c, xg[g], 0], zlate.at[0, g], right)
        got(r.at[v_far, c, xg[g], 1], yr.at[0, g])
        same(r.at[v_far, c, xg[g], 1], zlate.at[1, g], left)

    far(0)
    far(1)
    ring_step(1, xo, 1)
    swapped(1, v_z)
    rollout_part(v_z, False)
    far(2)
    far(3)
    swap(4, v_far)
    ring_step(1, xo, 2)
    swapped(2, v_up)
    rollout_part(v_up, False)
    swapped(3, v_dn)
    rollout_part(v_dn, False)
    trainer_part(x, xo)
    for n in range(2, 8):
        side = (n - 2) % 2
        k = (n - 2) // 2
        got(ring_block(xm, side, k), tx.at[0, n])
        got(ring_block(xp, side, k), tx.at[1, n])
    trainer_part(xm, xp)

    def train_stats(xx, carry):
        local_stats(lt, stat_t, xx, (xx,))
        return carry
    lax.fori_loop(0, NX, train_stats, 0)

    swapped(4, v_far)
    rollout_part(v_far, False)
    for g in range(4):
        got(r.at[w_up, c, xg[g]], ry.at[1, 1, g])
        got(r.at[w_dn, c, xg[g]], ry.at[0, 1, g])
    swap(5, w_up)
    swap(6, w_dn)
    for g in range(4):
        got(r.at[w_far, c, xg[g], 0], zlate.at[0, g])
        got(r.at[w_far, c, xg[g], 1], zlate.at[1, g])
    swap(7, w_far)
    swapped(5, w_up)
    rollout_part(w_up, False)
    swapped(6, w_dn)
    rollout_part(w_dn, False)
    swapped(7, w_far)
    rollout_part(w_far, False)

    def roll_stats(xx, carry):
        local_stats(lr, stat_r, xx, (pl.ds(pl.multiple_of(xx * GROUP, GROUP), GROUP),))
        return carry
    lax.fori_loop(0, NX, roll_stats, 0)

    for n in range(2):
        a1[0, 0, n] = stat_r[:, n, :]
        a1[0, 1, n] = stat_t[:, n, :]

    def exchange(buf, count, sem, to):
        def start(d, carry):
            pltpu.make_async_remote_copy(
                src_ref=buf.at[0], dst_ref=buf.at[d], send_sem=a_sem.at[sem], recv_sem=a_sem.at[sem + 1],
                device_id=to(d), device_id_type=MESH).start()
            return carry
        lax.fori_loop(1, count, start, 0)
        rest = buf.at[pl.ds(1, count - 1)]
        done = pltpu.make_async_remote_copy(
            src_ref=rest, dst_ref=rest, send_sem=a_sem.at[sem], recv_sem=a_sem.at[sem + 1],
            device_id=partner, device_id_type=MESH)
        done.wait_recv()
        return done

    def merge(buf, count):
        top = buf[0, :, 0]
        for d in range(1, count):
            top = jnp.maximum(top, buf[d, :, 0])
        total = jnp.zeros_like(top)
        for d in range(count):
            total = total + buf[d, :, 1] * jnp.exp(buf[d, :, 0] - top)
        return top, total

    done1 = exchange(a1, 16, 0, lambda d: dev(dx=d // 4, dy=d % 4))
    top, total = merge(a1, 16)
    a2[0, :, 0] = top
    a2[0, :, 1] = total
    done2 = exchange(a2, 8, 2, lambda d: dev(dz=d))
    top, total = merge(a2, 8)
    fin[:, 0] = top
    fin[:, 1] = total

    def compare(xx, carry):
        rows = pl.ds(pl.multiple_of(xx * GROUP, GROUP), GROUP)
        scale_r = jnp.exp(stat_r[xx, 0:1, :] - fin[0, 0, pl.ds(xx, 1), :]) / fin[0, 1, pl.ds(xx, 1), :]
        scale_t = jnp.exp(stat_t[xx, 0:1, :] - fin[1, 0, pl.ds(xx, 1), :]) / fin[1, 1, pl.ds(xx, 1), :]
        scale_r = jnp.sum(jnp.where(diagonal, scale_r, 0.0), axis=1, keepdims=True)
        scale_t = jnp.sum(jnp.where(diagonal, scale_t, 0.0), axis=1, keepdims=True)
        shared = jnp.zeros((GROUP, 1), F32)
        squares = jnp.zeros((GROUP, 1), F32)
        for n in range(2):
            p = lr[n, rows] * scale_r
            q = lt[n, xx] * scale_t
            shared = shared + jnp.sum(jnp.minimum(p, q), axis=1, keepdims=True)
            squares = squares + jnp.sum((q - p) * (q - p), axis=1, keepdims=True)
        table = jnp.where(lane == 0, shared, jnp.where(lane == 1, squares, 0.0))
        table = jnp.transpose(table)[:2]
        values = (table[0:1], table[1:2], stat_r[xx, 2:3, :], stat_t[xx, 2:3, :])
        part = lax.broadcasted_iota(jnp.int32, (1, 128), 1) // ROWS
        for zz in range(NH):
            line = jnp.zeros((1, 128), F32)
            for k in range(4):
                line = line + jnp.where(part == k, pltpu.roll(values[k], ((k - zz) % 4) * ROWS, 1), 0.0)
            out2[xx, zz] = line
        return carry
    lax.fori_loop(0, NX, compare, 0)

    a3[0] = out2[x, zh]

    def send(d, carry):
        dx, dy, dz = d // 32, (d // 8) % 4, d % 8
        pltpu.make_async_remote_copy(
            src_ref=out2.at[(x + dx) % NX, ((z + dz) % NZ) // 2], dst_ref=a3.at[d],
            send_sem=a_sem.at[4], recv_sem=a_sem.at[5], device_id=dev(dx, dy, dz), device_id_type=MESH).start()
        return carry
    lax.fori_loop(1, 128, send, 0)
    rest = a3.at[pl.ds(1, 127)]
    done3 = pltpu.make_async_remote_copy(
        src_ref=rest, dst_ref=rest, send_sem=a_sem.at[4], recv_sem=a_sem.at[5],
        device_id=partner, device_id_type=MESH)
    for cp in sends:
        cp.wait_send()
    done1.wait_send()
    done2.wait_send()
    done3.wait_recv()
    sums = jnp.sum(a3[...], axis=0)
    shift = (NH - zh) % NH * ROWS
    own_top = [pltpu.roll(fin[n, 0, pl.ds(x, 1), :], shift, 1)[:, :ROWS] for n in range(2)]
    own_total = [pltpu.roll(fin[n, 1, pl.ds(x, 1), :], shift, 1)[:, :ROWS] for n in range(2)]
    mask = mask_in[...].astype(F32)
    pick_r = pltpu.roll(sums, 2 * ROWS, 1)[:, :ROWS]
    pick_t = pltpu.roll(sums, ROWS, 1)[:, :ROWS]
    squares = pltpu.roll(sums, 3 * ROWS, 1)[:, :ROWS]
    log_ratio = pick_t - own_top[1] - jnp.log(own_total[1]) - (pick_r - own_top[0] - jnp.log(own_total[0]))
    shared_out[...] = sums[:, :ROWS] * mask
    dist_out[...] = jnp.sqrt(squares + 1e-06) * mask
    ratio_out[...] = jnp.minimum(jnp.exp(log_ratio), 2.0) * mask
    done3.wait_send()


def per_device(rollout_hidden, trainer_hidden, head_weight, token_ids, response_mask, trainer_slot):
    zh = (lax.axis_index("seq") // 2) % 4
    here = jnp.arange(NH, dtype=jnp.int32) == zh
    slots = jnp.where(here[None, :, None], trainer_slot.reshape(2, 1, HALF), 0).reshape(1, 128)
    ids = jnp.where(here[:, None], token_ids.reshape(1, ROWS), 0).reshape(1, 128)
    meta = jnp.concatenate([slots, ids], axis=0)
    dma, reg = pltpu.SemaphoreType.DMA, pl.BlockSpec(memory_space=pl.ANY)
    vmem = pl.BlockSpec(memory_space=pltpu.VMEM)
    outs = pl.pallas_call(
        kernel,
        out_shape=[jax.ShapeDtypeStruct((1, ROWS), F32)] * 3,
        in_specs=[reg, reg, reg, reg, vmem],
        out_specs=[vmem] * 3,
        scratch_shapes=[
            pltpu.VMEM((2, D, COLS), BF16),
            pltpu.VMEM((NX, NH, 2, HALF, D), BF16),
            pltpu.VMEM((8, 2, NX, 2, NH, HALF, FEAT), BF16),
            pltpu.VMEM((2, NX, NH, 2, 128), jnp.int32),
            pltpu.VMEM((TOK, 2 * TOK), BF16),
            pltpu.VMEM((TOK, FEAT), BF16),
            pltpu.VMEM((2, NX, GROUP, COLS), F32),
            pltpu.VMEM((2, TOK, COLS), F32),
            pltpu.VMEM((NX, 8, 128), F32),
            pltpu.VMEM((NX, 8, 128), F32),
            pltpu.VMEM((16, 2, 2, NX, 128), F32),
            pltpu.VMEM((8, 2, 2, NX, 128), F32),
            pltpu.VMEM((2, 2, NX, 128), F32),
            pltpu.VMEM((NX, NH, 1, 128), F32),
            pltpu.VMEM((128, 1, 128), F32),
            dma((128,)), dma((4,)), dma,
            dma((2, 9)), dma((2, 2, 3)), dma((3,)), dma((3,)), dma((2, 2)), dma((3,)), dma,
            dma((2, 2, 4)), dma((2, 4)), dma((2, 4)), dma((2, 4)), dma((8,)), dma((6,)),
        ],
        compiler_params=pltpu.CompilerParams(
            collective_id=0, has_side_effects=True, vmem_limit_bytes=60 * 1024 * 1024),
        cost_estimate=pl.CostEstimate(
            flops=2 * 2 * TOK * D * 2 * COLS + 2 * TOK * 2 * TOK * D, bytes_accessed=D * COLS * 2, transcendentals=2 * TOK * 2 * COLS),
    )(rollout_hidden.reshape(2, HALF, FEAT), trainer_hidden.reshape(2, HALF, D), head_weight, meta,
      response_mask.reshape(1, ROWS))
    return tuple(o.reshape(ROWS) for o in outs)


def solution(mesh):
    placed = (
        P("seq", "vocab"),
        P("seq", None),
        P(None, ("seq", "vocab")),
        P("seq"),
        P("seq"),
        P("seq"),
    )
    return jax.shard_map(
        per_device,
        mesh=mesh,
        in_specs=placed,
        out_specs=(P("seq"), P("seq"), P("seq")),
        check_vma=False,
    )
```

```python
import jax
import jax.numpy as jnp
from jax import lax
from jax.experimental import pallas as pl
from jax.experimental.pallas import tpu as pltpu
from jax.sharding import PartitionSpec as P

MESH = pl.DeviceIdType.MESH
BF16 = jnp.bfloat16
F32 = jnp.float32
NX, NY, NZ, NH = 4, 4, 8, 4
ROWS = 32
HALF = 16
D = 4096
FEAT = 512
COLS = 592
TOK = 512
GROUP = 128
PART = 1024
ARRIVALS = 86

ORDER = (
    ("start", 0), ("fx", 1), ("tzown", 1), ("fx", 3), ("tzown", 0), ("sx", 0),
    ("sx", 1), ("fx", 0), ("head", 0), ("tzown", 3), ("sx", 2), ("sz", 1),
    ("tl", 1), ("tr", 1), ("tzown", 2), ("near0", 1), ("sz", 0), ("spread", 0),
    ("meta1", 0), ("sz", 2), ("tr", 0), ("tl", 0), ("near0", 0), ("s2r", 1),
    ("s2l", 1), ("near0", 3), ("fx", 10), ("own1", 1), ("own1", 3), ("relayu", 0),
    ("relayd", 0), ("near0", 2), ("fx", 8), ("meta2", 0), ("away0", 1), ("cross", 0),
    ("fx", 4), ("own1", 2), ("near1", 1), ("onehot", 0), ("s2l", 0), ("fx", 5),
    ("own1", 0), ("s3", 1), ("near1", 3), ("s2r", 0), ("fx", 6), ("away0", 0),
    ("near0", 5), ("s2r", 2), ("s2l", 2), ("spread", 2), ("fx", 9), ("near1", 2),
    ("away1", 1), ("fx", 14), ("s3", 0), ("near1", 0), ("fx", 2), ("relayu", 2),
    ("relayd", 2), ("swap", 0), ("s3", 2), ("spread", 3), ("relayu", 1), ("relayd", 1),
    ("fx", 12), ("spread", 1), ("cross", 2), ("fx", 15), ("R", 0), ("near0", 4),
    ("away1", 0), ("fx", 7), ("swap", 2), ("swap", 3), ("T", 2), ("far", 1),
    ("relayd", 3), ("relayu", 3), ("fx", 11), ("near1", 5), ("R", 2), ("near1", 4),
    ("swap", 1), ("cross", 1), ("R", 3), ("far", 2), ("fx", 13), ("cross", 3),
    ("swap", 4), ("T", 3), ("far", 3), ("R", 1), ("far", 0), ("T", 1),
    ("R", 4), ("swap", 5), ("swap", 6), ("T", 0), ("TS", 0), ("swap", 7),
    ("R", 5), ("R", 6), ("R", 7), ("RS", 0),
)


def kernel(roll_in, train_in, head_in, slot_in, ids_in, out,
           w, t, r, slot_v, ids_v, line, meta, onehot, perm, lt, lr, stat_r, stat_t, a1, a2, fin, out2, a3,
           ssem, rsem, in_sem, a_sem):
    s, v = lax.axis_index("seq"), lax.axis_index("vocab")
    x, zh, c = s // 8, (s // 2) % 4, s % 2
    zl, y = v // 4, v % 4
    z = zh * 2 + zl

    def dev(dx=0, dy=0, dz=0):
        xx, yy, zz = (x + dx + NX) % NX, (y + dy + NY) % NY, (z + dz + NZ) % NZ
        return ((xx * 4 + zz // 2) * 2 + c, (zz % 2) * 4 + yy)

    partner = (s + 1 - 2 * c, v)
    xm, xp, xo = (x + 3) % 4, (x + 1) % 4, (x + 2) % 4
    xg = (x, xm, xp, xo)
    zm, zp, zo = (zh + 3) % 4, (zh + 1) % 4, (zh + 2) % 4

    barrier = pltpu.get_barrier_semaphore()
    near = [dev(dz=d) for d in (4, 2, -2)] + [dev(dx=2)] + [dev(dx=d) for d in (1, -1)]
    near += [dev(dy=d) for d in (1, -1)] + [dev(dz=d) for d in (1, -1)] + [partner]
    for to in near:
        pl.semaphore_signal(barrier, inc=1, device_id=to, device_id_type=MESH)

    copies = [
        pltpu.make_async_copy(slot_in, slot_v, in_sem.at[6]),
        pltpu.make_async_copy(ids_in, ids_v, in_sem.at[7]),
        pltpu.make_async_copy(roll_in, r.at[v, c, x, :, zh], in_sem.at[0]),
    ]
    for q in range(4):
        copies.append(pltpu.make_async_copy(train_in.at[:, q * PART:(q + 1) * PART], t.at[x, zh, q], in_sem.at[1 + q]))
    copies.append(pltpu.make_async_copy(head_in, w.at[:COLS], in_sem.at[5]))
    for cp in copies:
        cp.start()
    for cp in copies[:2]:
        cp.wait()
    lanes = lax.broadcasted_iota(jnp.int32, (1, 128), 1)
    line[0:1, :ROWS] = slot_v[...]
    line[1:2, :ROWS] = ids_v[...]
    slots, ids = line[0:1, :], line[1:2, :]
    low = jnp.where(lanes // HALF == zh, pltpu.roll(slots, zh * HALF, 1), 0)
    high = jnp.where(lanes // HALF == NH + zh, pltpu.roll(slots, (NH - 1 + zh) * HALF, 1), 0)
    meta[c, x, zh, 0:1, :] = low + high
    meta[c, x, zh, 1:2, :] = jnp.where(lanes // ROWS == zh, pltpu.roll(ids, zh * ROWS, 1), 0)
    for cp in copies[2:7]:
        cp.wait()
    pl.semaphore_wait(barrier, len(near))

    right, left = dev(dz=1), dev(dz=-1)
    outward, inward = dev(dz=2 * zl - 1), dev(dz=1 - 2 * zl)
    xr, xl = dev(dx=1), dev(dx=-1)
    yu, yd = dev(dy=1), dev(dy=-1)
    z_near, z_away = (1 - zl) * zm + zl * zp, (1 - zl) * zp + zl * zm
    zz = (zm, zp, zo)

    v_z = (1 - zl) * 4 + y
    v_up, v_dn, v_far = zl * 4 + (y + 1) % 4, zl * 4 + (y + 3) % 4, zl * 4 + (y + 2) % 4
    w_up, w_dn, w_far = (1 - zl) * 4 + (y + 1) % 4, (1 - zl) * 4 + (y + 3) % 4, (1 - zl) * 4 + (y + 2) % 4
    features = (v, v_z, v_dn, v_up, v_far, w_dn, w_up, w_far)

    block = {}

    def small(vv, xx, zq):
        return r.at[vv, c, xx, :, zq]

    for k in range(3):
        block["sz", k] = small(v, x, zz[k])
        block["sx", k] = small(v, (xm, xp, xo)[k], zh)
        block["mz", k] = meta.at[c, x, zz[k]]
        block["mx", k] = meta.at[c, (xm, xp, xo)[k]]
        block["s2l", k] = small(v, xm, zz[k])
        block["s2r", k] = small(v, xp, zz[k])
        block["s3l", k] = r.at[v, c, xo, 0, zz[k]]
        block["s3r", k] = r.at[v, c, xo, 1, zz[k]]
    block["ms", 0] = meta.at[1 - c]
    block["w", 0] = w.at[COLS:]
    order = [(x, zh)] + [(x, q) for q in zz] + [(xx, zh) for xx in xg[1:]] + [(xx, q) for xx in xg[1:] for q in zz]
    for k, (xx, zq) in enumerate(order):
        block["yu", k] = small(v_dn, xx, zq)
        block["yd", k] = small(v_up, xx, zq)
    for g in range(4):
        block["rr", g] = r.at[v_z, c, xg[g], 0]
        block["rl", g] = r.at[v_z, c, xg[g], 1]
        block["cu", g] = r.at[w_dn, c, xg[g]]
        block["cd", g] = r.at[w_up, c, xg[g]]
        block["fu", g] = r.at[v_far, c, xg[g], 1]
        block["fd", g] = r.at[v_far, c, xg[g], 0]
        block["lr", g] = r.at[w_far, c, xg[g], 0]
        block["ll", g] = r.at[w_far, c, xg[g], 1]
    for k in range(8):
        block["v", k] = r.at[features[k], 1 - c]

    def qn(k):
        return zl * (3 - k) + (1 - zl) * k

    def qf(k):
        return zl * k + (1 - zl) * (3 - k)

    def near_block(xx, k):
        return t.at[xx, z_near if k < 4 else zo, qn(k % 4)]

    def away_block(xx, k):
        return t.at[xx, z_away if k < 4 else zo, qf(k % 4)]

    quarter = {}
    for k in range(6):
        for g, xx in enumerate((x, xo)):
            block["tn%d" % g, k] = near_block(xx, k)
            block["tf%d" % g, k] = away_block(xx, k)
            quarter["tn%d" % g, k] = 3 - k % 4
            quarter["tf%d" % g, k] = k % 4
        for name, xx in (("tl", xm), ("tr", xp)):
            block[name, 4 + 2 * k] = near_block(xx, k)
            block[name, 5 + 2 * k] = away_block(xx, k)
            quarter[name, 4 + 2 * k] = 3 - k % 4
            quarter[name, 5 + 2 * k] = k % 4
    for k in range(4):
        block["tl", k] = t.at[xm, zh, qf(k)]
        block["tr", k] = t.at[xp, zh, qf((k + 2) % 4)]
        quarter["tl", k] = k
        quarter["tr", k] = (k + 2) % 4
    for k in range(2):
        block["ul", k] = t.at[xo, zh, qf(k)]
        block["ur", k] = t.at[xo, zh, qf(k + 2)]
        quarter["ul", k] = k
        quarter["ur", k] = k + 2
    def wait_key(name, k):
        if name in ("yu", "yd"):
            g = [n for n in range(4) if k in members[n]][0]
            return (name, g), r.at[v_dn if name == "yu" else v_up, c, xg[g]]
        if name in ("rr", "rl"):
            return ("rr", k), r.at[v_z, c, xg[k]]
        if name in ("fu", "fd"):
            return ("fu", k), r.at[v_far, c, xg[k]]
        if name in ("s3l", "s3r"):
            return ("s3l", k), small(v, xo, zz[k])
        if name in ("cu", "cd"):
            return (name, 0), r.at[w_dn if name == "cu" else w_up, c]
        if name in ("lr", "ll"):
            return ("lr", 0), r.at[w_far, c]
        if name == "mz":
            return (name, 0), meta.at[c, x, pl.ds(0, 3)]
        if name == "mx":
            return (name, 0), meta.at[c, pl.ds(0, 3)]
        if name in ("tl", "tr") and k >= 4:
            return ("tq", quarter[name, k]), t.at[0, pl.ds(0, 3), pl.ds(0, 2)]
        return (name, k), block[name, k]

    members = ((0, 1, 2, 3), (4, 7, 8, 9), (5, 10, 11, 12), (6, 13, 14, 15))
    wait_of = {name: wait_key(*name) for name in block}
    keys = {}
    for key, _ in wait_of.values():
        keys.setdefault(key, len(keys))
    assert len(keys) == ARRIVALS, len(keys)

    sent = {n: 0 for n in range(11)}
    waited = set()

    def send_sem(name):
        if name in ("v", "w"):
            n = 0 if name == "v" else 1
        elif name in ("rr", "rl", "cu", "cd", "fu", "fd", "lr", "ll"):
            n = 4
        elif name in ("s3l", "s3r"):
            n = 7
        elif name in ("mz", "mx", "ms"):
            n = 8 + ("mz", "mx", "ms").index(name)
        elif name in ("sz", "sx", "s2l", "s2r", "yu", "yd"):
            n = 5 if sent[5] < 32 else 6
        else:
            n = 2 if sent[2] < 48 else 3
        sent[n] += 1
        return n

    def put(name, n, ref, to, dst=None):
        pltpu.make_async_remote_copy(
            src_ref=ref, dst_ref=ref if dst is None else dst, send_sem=ssem.at[send_sem(name)],
            recv_sem=rsem.at[keys[wait_of[name, n][0]]], device_id=to, device_id_type=MESH).start()

    def all_sent():
        whole_sends = (
            r.at[:, 0], w.at[:COLS], t.at[pl.ds(0, 3)], t.at[0, pl.ds(0, 3)], r.at[pl.ds(0, 5), 0],
            r.at[:, 0, :, :, 0], r.at[pl.ds(0, 3), 0, :, :, 0], r.at[pl.ds(0, 3), 0, 0, :, 0],
            meta.at[0, 0, pl.ds(0, 3)], meta.at[0, pl.ds(0, 3)], meta.at[0],
        )
        assert tuple(sent.values()) == (8, 1, 48, 12, 32, 32, 12, 6, 3, 3, 1), sent
        for n, ref in enumerate(whole_sends):
            pltpu.make_async_remote_copy(
                src_ref=ref, dst_ref=ref, send_sem=ssem.at[n], recv_sem=ssem.at[n],
                device_id=partner, device_id_type=MESH).wait_send()

    def need(*names):
        for name in names:
            key, ref = wait_of[name]
            if key not in waited:
                waited.add(key)
                sem = rsem.at[keys[key]]
                pltpu.make_async_remote_copy(
                    src_ref=ref, dst_ref=ref, send_sem=sem, recv_sem=sem,
                    device_id=partner, device_id_type=MESH).wait_recv()

    def up_down(k, ref):
        put("yu", k, ref, yu)
        put("yd", k, ref, yd)

    own = small(v, x, zh)
    of_group = (
        [("sz", k) for k in range(3)],
        [("sx", 0)] + [("s2l", k) for k in range(3)],
        [("sx", 1)] + [("s2r", k) for k in range(3)],
        [("sx", 2)] + [(a, k) for a in ("s3l", "s3r") for k in range(3)],
    )
    whole = (
        sum(of_group, []),
        [(a, g) for a in ("rr", "rl") for g in range(4)],
        [("yu", k) for k in range(16)],
        [("yd", k) for k in range(16)],
        [(a, g) for a in ("fu", "fd") for g in range(4)],
        [("cu", g) for g in range(4)],
        [("cd", g) for g in range(4)],
        [(a, g) for a in ("lr", "ll") for g in range(4)],
    )

    def do(task, k):
        if task == "start":
            for n, d in enumerate((2, -2, 4)):
                put("sz", n, own, dev(dz=d))
            for n, d in enumerate((1, -1, 2)):
                put("sx", n, own, dev(dx=d))
            up_down(0, own)
            for n, d in enumerate((2, -2, 4)):
                put("mz", n, meta.at[c, x, zh], dev(dz=d))
        elif task == "head":
            copies[7].wait()
            put("w", 0, w.at[:COLS], partner, w.at[COLS:])
        elif task == "fx" and k < 4:
            put("tl", k, t.at[x, zh, qf(k)], xr)
            put("tr", k, t.at[x, zh, qf((k + 2) % 4)], xl)
        elif task == "fx":
            name = ("tf0", (k - 5) // 2) if k % 2 else ("tn0", (k - 4) // 2)
            need(name)
            put("tl", k, block[name], xr)
            put("tr", k, block[name], xl)
        elif task == "tzown":
            put("tn0", k, t.at[x, zh, qf(k)], outward)
        elif task == "meta1":
            need(("mz", 0), ("mz", 1), ("mz", 2))
            for n, d in enumerate((1, -1, 2)):
                put("mx", n, meta.at[c, x], dev(dx=d))
        elif task == "meta2":
            need(("mx", 0), ("mx", 1), ("mx", 2))
            put("ms", 0, meta.at[c], partner)
        elif task == "sz":
            need(("sz", k))
            ref = block["sz", k]
            put("s2l", k, ref, xr)
            put("s2r", k, ref, xl)
            up_down(1 + k, ref)
        elif task == "sx":
            need(("sx", k))
            up_down(4 + k, block["sx", k])
        elif task == "s2l":
            need(("s2l", k))
            put("s3l", k, r.at[v, c, xm, 0, zz[k]], xr)
            up_down(7 + k, block["s2l", k])
        elif task == "s2r":
            need(("s2r", k))
            put("s3r", k, r.at[v, c, xp, 1, zz[k]], xl)
            up_down(10 + k, block["s2r", k])
        elif task == "s3":
            need(("s3l", k), ("s3r", k))
            up_down(13 + k, small(v, xo, zz[k]))
        elif task == "spread":
            need(*of_group[k])
            put("rr", k, r.at[v, c, xg[k], 0], right)
            put("rl", k, r.at[v, c, xg[k], 1], left)
        elif task == "cross":
            need(("rr", k), ("rl", k))
            put("cu", k, r.at[v_z, c, xg[k]], yu)
            put("cd", k, r.at[v_z, c, xg[k]], yd)
        elif task == "relayu":
            need(*[("yu", i) for i in members[k]])
            put("fu", k, r.at[v_dn, c, xg[k], 1], yu)
        elif task == "relayd":
            need(*[("yd", i) for i in members[k]])
            put("fd", k, r.at[v_up, c, xg[k], 0], yd)
        elif task == "far":
            need(("fu", k), ("fd", k))
            put("lr", k, r.at[v_far, c, xg[k], 0], right)
            put("ll", k, r.at[v_far, c, xg[k], 1], left)
        elif task == "swap":
            need(*whole[k])
            put("v", k, r.at[features[k], c], partner)
        elif task in ("near0", "near1"):
            g = task[-1]
            need(("tn" + g, k))
            ref = block["tn" + g, k]
            put("tf" + g, k, ref, inward)
        elif task in ("away0", "away1"):
            g = task[-1]
            need(("tf" + g, k))
            put("tn" + g, 4 + k, block["tf" + g, k], outward)
        elif task == "tl":
            need(("tl", k))
            put("ul", k, block["tl", k], xr)
        elif task == "tr":
            need(("tr", k))
            put("ur", k, block["tr", k], xl)
        elif task == "own1":
            name = ("ul", k) if k < 2 else ("ur", k - 2)
            need(name)
            put("tn1", k, block[name], outward)
        elif task == "R":
            need(("v", k), ("w", 0), *whole[k])
            rollout_part(features[k])
        elif task == "T":
            need(("w", 0), *[name for name, q in quarter.items() if q == k])
            trainer_part(qf(k))
        elif task == "onehot":
            need(("ms", 0))
            fill_onehot()
        elif task == "TS":
            lax.fori_loop(0, NX, train_stats, 0)
        elif task == "RS":
            lax.fori_loop(0, NX, roll_stats, 0)

    def fill_onehot():
        place = lax.broadcasted_iota(jnp.int32, (TOK, GROUP), 0)
        for cc in range(2):
            for xx in range(NX):
                slot = meta[cc, xx, 0, 0:1, :]
                for zq in range(1, NH):
                    slot = slot + meta[cc, xx, zq, 0:1, :]
                token = (slot >> 6) * ROWS + (slot & (ROWS - 1))
                token = jnp.where(((slot >> 5) & 1) == c, token, -1)
                n = cc * NX + xx
                onehot[:, n * GROUP:(n + 1) * GROUP] = jnp.where(place == token, 1.0, 0.0).astype(BF16)

    def logits(rows, f):
        return lax.dot_general(rows, w[:, f], (((1,), (1,)), ((), ())), preferred_element_type=F32)

    begun = set()

    def add(logit, part):
        if id(logit) in begun:
            logit[...] += part
        else:
            begun.add(id(logit))
            logit[...] = part

    def rollout_part(vv):
        rows = r[vv].reshape(2 * TOK, FEAT)
        perm[...] = jnp.dot(onehot[...], rows, preferred_element_type=F32).astype(BF16)
        add(lr, logits(perm[...], pl.ds(pl.multiple_of(vv * FEAT, FEAT), FEAT)))

    def trainer_part(q):
        rows = t[:, :, pl.ds(q, 1)].reshape(TOK, PART)
        add(lt, logits(rows, pl.ds(pl.multiple_of(q * PART, PART), PART)))

    lane = lax.broadcasted_iota(jnp.int32, (GROUP, 128), 1)
    column = lax.broadcasted_iota(jnp.int32, (GROUP, 2 * COLS), 1)
    column = column + jnp.where(column < COLS, (s * 8 + v) * COLS, ((s + 1 - 2 * c) * 8 + v) * COLS - COLS)
    diagonal = lax.broadcasted_iota(jnp.int32, (GROUP, 128), 0) == lane

    def local_stats(logit, stat, xx, rows):
        ids = meta[c, xx, 0, 1:2, :]
        for zq in range(1, NH):
            ids = ids + meta[c, xx, zq, 1:2, :]
        ids = jnp.sum(jnp.where(diagonal, ids, 0), axis=1, keepdims=True)
        values = logit[rows]
        top = jnp.max(values, axis=1, keepdims=True)
        e = jnp.exp(values - top)
        logit[rows] = e
        total = jnp.sum(e, axis=1, keepdims=True)
        pick = jnp.sum(jnp.where(column == ids, values, 0.0), axis=1, keepdims=True)
        table = jnp.where(lane == 0, top, jnp.where(lane == 1, total, jnp.where(lane == 2, pick, 0.0)))
        stat[xx] = jnp.transpose(table)[:8]

    rows_of = lambda xx: pl.ds(pl.multiple_of(xx * GROUP, GROUP), GROUP)

    def train_stats(xx, carry):
        local_stats(lt, stat_t, xx, rows_of(xx))
        return carry

    def roll_stats(xx, carry):
        local_stats(lr, stat_r, xx, rows_of(xx))
        return carry

    def exchange(buf, count, sem, to):
        def start(d, carry):
            pltpu.make_async_remote_copy(
                src_ref=buf.at[0], dst_ref=buf.at[d], send_sem=a_sem.at[sem], recv_sem=a_sem.at[sem + 1],
                device_id=to(d), device_id_type=MESH).start()
            return carry
        lax.fori_loop(1, count, start, 0)
        rest = buf.at[pl.ds(1, count - 1)]
        return pltpu.make_async_remote_copy(
            src_ref=rest, dst_ref=rest, send_sem=a_sem.at[sem], recv_sem=a_sem.at[sem + 1],
            device_id=partner, device_id_type=MESH)

    def merge(buf, count):
        top = buf[0, 0]
        for d in range(1, count):
            top = jnp.maximum(top, buf[d, 0])
        total = jnp.zeros_like(top)
        for d in range(count):
            total = total + buf[d, 1] * jnp.exp(buf[d, 0] - top)
        return top, total

    def plane(n, stat):
        a1[n, 0, 0] = stat[:, 0, :]
        a1[n, 0, 1] = stat[:, 1, :]
        return exchange(a1.at[n], 16, 4 * n, lambda d: dev(dx=d // 4, dy=d % 4))

    def column_z(n, before):
        before.wait_recv()
        top, total = merge(a1.at[n], 16)
        a2[n, 0, 0] = top
        a2[n, 0, 1] = total
        return exchange(a2.at[n], 8, 4 * n + 2, lambda d: dev(dz=d))

    def finish(n, before):
        before.wait_recv()
        top, total = merge(a2.at[n], 8)
        fin[n, 0] = top
        fin[n, 1] = total

    for task, k in ORDER:
        do(task, k)
        if task == "TS":
            plane_t = plane(1, stat_t)
    plane_r = plane(0, stat_r)
    column_t = column_z(1, plane_t)
    column_r = column_z(0, plane_r)
    finish(1, column_t)
    finish(0, column_r)

    def compare(xx, carry):
        rows = pl.ds(pl.multiple_of(xx * GROUP, GROUP), GROUP)
        scale_r = jnp.exp(stat_r[xx, 0:1, :] - fin[0, 0, pl.ds(xx, 1), :]) / fin[0, 1, pl.ds(xx, 1), :]
        scale_t = jnp.exp(stat_t[xx, 0:1, :] - fin[1, 0, pl.ds(xx, 1), :]) / fin[1, 1, pl.ds(xx, 1), :]
        scale_r = jnp.sum(jnp.where(diagonal, scale_r, 0.0), axis=1, keepdims=True)
        scale_t = jnp.sum(jnp.where(diagonal, scale_t, 0.0), axis=1, keepdims=True)
        p = lr[rows, :] * scale_r
        q = lt[rows, :] * scale_t
        shared = jnp.sum(jnp.minimum(p, q), axis=1, keepdims=True)
        squares = jnp.sum((q - p) * (q - p), axis=1, keepdims=True)
        table = jnp.where(lane == 0, shared, jnp.where(lane == 1, squares, 0.0))
        table = jnp.transpose(table)[:2]
        values = (table[0:1], table[1:2], stat_r[xx, 2:3, :], stat_t[xx, 2:3, :])
        part = lax.broadcasted_iota(jnp.int32, (1, 128), 1) // ROWS
        for zq in range(NH):
            one = jnp.zeros((1, 128), F32)
            for k in range(4):
                one = one + jnp.where(part == k, pltpu.roll(values[k], ((k - zq) % 4) * ROWS, 1), 0.0)
            out2[xx, zq] = one
        return carry
    lax.fori_loop(0, NX, compare, 0)

    a3[0] = out2[x, zh]

    def send(d, carry):
        dx, dy, dz = d // 32, (d // 8) % 4, d % 8
        pltpu.make_async_remote_copy(
            src_ref=out2.at[(x + dx) % NX, ((z + dz) % NZ) // 2], dst_ref=a3.at[d],
            send_sem=a_sem.at[8], recv_sem=a_sem.at[9], device_id=dev(dx, dy, dz), device_id_type=MESH).start()
        return carry
    lax.fori_loop(1, 128, send, 0)
    rest = a3.at[pl.ds(1, 127)]
    done3 = pltpu.make_async_remote_copy(
        src_ref=rest, dst_ref=rest, send_sem=a_sem.at[8], recv_sem=a_sem.at[9],
        device_id=partner, device_id_type=MESH)
    all_sent()
    for done in (plane_t, plane_r, column_t, column_r):
        done.wait_send()
    done3.wait_recv()
    sums = jnp.sum(a3[...], axis=0)
    shift = (NH - zh) % NH * ROWS
    own_top = [pltpu.roll(fin[n, 0, pl.ds(x, 1), :], shift, 1)[:, :ROWS] for n in range(2)]
    own_total = [pltpu.roll(fin[n, 1, pl.ds(x, 1), :], shift, 1)[:, :ROWS] for n in range(2)]
    pick_r = pltpu.roll(sums, 2 * ROWS, 1)[:, :ROWS]
    pick_t = pltpu.roll(sums, ROWS, 1)[:, :ROWS]
    squares = pltpu.roll(sums, 3 * ROWS, 1)[:, :ROWS]
    log_ratio = pick_t - own_top[1] - jnp.log(own_total[1]) - (pick_r - own_top[0] - jnp.log(own_total[0]))
    out[0:1, :] = sums[:, :ROWS]
    out[1:2, :] = jnp.sqrt(squares + 1e-06)
    out[2:3, :] = jnp.minimum(jnp.exp(log_ratio), 2.0)
    done3.wait_send()


def per_device(rollout_hidden, trainer_hidden, head_weight, token_ids, response_mask, trainer_slot):
    dma, reg = pltpu.SemaphoreType.DMA, pl.BlockSpec(memory_space=pl.ANY)
    vmem = pl.BlockSpec(memory_space=pltpu.VMEM)
    sums = pl.pallas_call(
        kernel,
        out_shape=jax.ShapeDtypeStruct((3, ROWS), F32),
        in_specs=[reg] * 5,
        out_specs=vmem,
        scratch_shapes=[
            pltpu.VMEM((2 * COLS, D), BF16),
            pltpu.VMEM((NX, NH, 4, ROWS, PART), BF16),
            pltpu.VMEM((8, 2, NX, 2, NH, HALF, FEAT), BF16),
            pltpu.VMEM((1, ROWS), jnp.int32),
            pltpu.VMEM((1, ROWS), jnp.int32),
            pltpu.VMEM((2, 128), jnp.int32),
            pltpu.VMEM((2, NX, NH, 2, 128), jnp.int32),
            pltpu.VMEM((TOK, 2 * TOK), BF16),
            pltpu.VMEM((TOK, FEAT), BF16),
            pltpu.VMEM((TOK, 2 * COLS), F32),
            pltpu.VMEM((TOK, 2 * COLS), F32),
            pltpu.VMEM((NX, 8, 128), F32),
            pltpu.VMEM((NX, 8, 128), F32),
            pltpu.VMEM((2, 16, 2, NX, 128), F32),
            pltpu.VMEM((2, 8, 2, NX, 128), F32),
            pltpu.VMEM((2, 2, NX, 128), F32),
            pltpu.VMEM((NX, NH, 1, 128), F32),
            pltpu.VMEM((128, 1, 128), F32),
            dma((11,)), dma((ARRIVALS,)), dma((8,)), dma((10,)),
        ],
        compiler_params=pltpu.CompilerParams(
            collective_id=0, has_side_effects=True, vmem_limit_bytes=60 * 1024 * 1024),
        cost_estimate=pl.CostEstimate(
            flops=2 * 2 * TOK * D * 2 * COLS + 2 * TOK * 2 * TOK * D, bytes_accessed=D * COLS * 2, transcendentals=2 * TOK * 2 * COLS),
    )(rollout_hidden.reshape(2, HALF, FEAT), trainer_hidden, head_weight.T,
      trainer_slot.reshape(1, ROWS), token_ids.reshape(1, ROWS))
    mask = response_mask.astype(F32)
    return tuple(sums[n] * mask for n in range(3))


def solution(mesh):
    placed = (
        P("seq", "vocab"),
        P("seq", None),
        P(None, ("seq", "vocab")),
        P("seq"),
        P("seq"),
        P("seq"),
    )
    return jax.shard_map(
        per_device,
        mesh=mesh,
        in_specs=placed,
        out_specs=(P("seq"), P("seq"), P("seq")),
        check_vma=False,
    )
```

```python
import jax
import jax.numpy as jnp
from jax import lax
from jax.experimental import pallas as pl
from jax.experimental.pallas import tpu as pltpu
from jax.sharding import PartitionSpec as P

MESH = pl.DeviceIdType.MESH
BF16 = jnp.bfloat16
F32 = jnp.float32
NX, NY, NZ, NH = 4, 4, 8, 4
ROWS = 32
HALF = 16
D = 4096
FEAT = 512
COLS = 592
WIDE = 1280
TOK = 512
GROUP = 128
PART = 1024
ARRIVALS = 86

ORDER = (
    ("fx", 0), ("start", 0), ("fx", 1), ("tzown", 0), ("fx", 3), ("tzown", 2),
    ("tl", 0), ("tr", 0), ("tzown", 1), ("sx", 0), ("yz", 0), ("head", 0),
    ("yz", 1), ("sx", 1), ("sz", 0), ("tzown", 3), ("sx", 2), ("sz", 1),
    ("near0", 0), ("tl", 1), ("tr", 1), ("spread", 0), ("yz", 2), ("near0", 2),
    ("meta1", 0), ("fx", 4), ("own1", 0), ("near0", 1), ("sz", 2), ("own1", 2),
    ("y2l", 0), ("y2r", 0), ("s2r", 0), ("s2l", 0), ("fx", 5), ("y2r", 1),
    ("near0", 3), ("y2l", 1), ("away0", 0), ("relayu", 0), ("relayd", 0), ("s2r", 1),
    ("s2l", 1), ("fx", 6), ("own1", 3), ("cross", 0), ("meta2", 0), ("near1", 0),
    ("fx", 9), ("own1", 1), ("onehot", 0), ("near1", 2), ("s2r", 2), ("s2l", 2),
    ("spread", 2), ("y2r", 2), ("fx", 7), ("s3", 0), ("near0", 4), ("away0", 1),
    ("y2l", 2), ("fx", 11), ("s3", 1), ("near1", 3), ("away1", 0), ("fx", 12),
    ("near1", 1), ("swap", 0), ("s3", 2), ("fx", 10), ("relayu", 2), ("relayd", 2),
    ("spread", 1), ("cross", 2), ("fx", 2), ("R", 0), ("swap", 2), ("relayu", 1),
    ("relayd", 1), ("fx", 13), ("spread", 3), ("near1", 4), ("swap", 3), ("T", 3),
    ("relayu", 3), ("near0", 5), ("relayd", 3), ("away1", 1), ("fx", 14), ("fx", 8),
    ("R", 2), ("far", 2), ("cross", 1), ("swap", 1), ("R", 3), ("far", 0),
    ("cross", 3), ("far", 1), ("T", 0), ("near1", 5), ("fx", 15), ("swap", 4),
    ("T", 2), ("far", 3), ("R", 1), ("R", 4), ("swap", 5), ("swap", 6),
    ("T", 1), ("TS", 0), ("swap", 7), ("R", 5), ("R", 6), ("R", 7),
    ("RS", 0),
)


def kernel(roll_in, train_in, head_in, slot_in, ids_in, out,
           w, t, r, slot_v, ids_v, line, meta, onehot, perm, lt, lr, et, er, stat_r, stat_t, a1, a2, fin, out2, a3,
           ssem, rsem, in_sem, a_sem):
    s, v = lax.axis_index("seq"), lax.axis_index("vocab")
    x, zh, c = lax.div(s, 8), lax.rem(lax.div(s, 2), 4), lax.rem(s, 2)
    zl, y = lax.div(v, 4), lax.rem(v, 4)
    z = zh * 2 + zl

    x_at = [lax.rem(x + d, NX) for d in range(NX)]
    y_at = [lax.rem(y + d, NY) for d in range(NY)]
    z_at = [lax.rem(z + d, NZ) for d in range(NZ)]
    zh_at = [lax.div(zz, 2) for zz in z_at]
    seq_x = [8 * xx + c for xx in x_at]
    seq_z = [2 * zz for zz in zh_at]
    vocab_z = [4 * lax.rem(zz, 2) for zz in z_at]

    def dev(dx=0, dy=0, dz=0):
        return (seq_x[dx % NX] + seq_z[dz % NZ], vocab_z[dz % NZ] + y_at[dy % NY])

    def offsets(xs, ys, zs):
        every = [(dx, dy, dz) for dx in range(xs) for dy in range(ys) for dz in range(zs)][1:]
        return sorted(every, key=lambda o: -min(o[0], NX - o[0]) - min(o[1], NY - o[1]) - min(o[2], NZ - o[2]))

    partner = (s + 1 - 2 * c, v)
    xm, xp, xo = x_at[3], x_at[1], x_at[2]
    xg = (x, xm, xp, xo)
    zm, zp, zo = zh_at[6], zh_at[2], zh_at[4]

    barrier = pltpu.get_barrier_semaphore()
    near = [dev(dz=d) for d in (4, 2, -2)] + [dev(dx=2)] + [dev(dx=d) for d in (1, -1)]
    near += [dev(dy=d) for d in (1, -1)] + [dev(dz=d) for d in (1, -1)] + [partner]
    for to in near:
        pl.semaphore_signal(barrier, inc=1, device_id=to, device_id_type=MESH)

    copies = [
        pltpu.make_async_copy(slot_in, slot_v, in_sem.at[6]),
        pltpu.make_async_copy(ids_in, ids_v, in_sem.at[7]),
        pltpu.make_async_copy(roll_in, r.at[v, c, x, :, zh], in_sem.at[0]),
    ]
    for q in range(4):
        copies.append(pltpu.make_async_copy(train_in.at[:, q * PART:(q + 1) * PART], t.at[x, zh, q], in_sem.at[1 + q]))
    copies.append(pltpu.make_async_copy(head_in, w.at[:COLS], in_sem.at[5]))
    for cp in copies:
        cp.start()
    for cp in copies[:2]:
        cp.wait()
    lanes = lax.broadcasted_iota(jnp.int32, (1, 128), 1)
    line[0:1, :ROWS] = slot_v[...]
    line[1:2, :ROWS] = ids_v[...]
    slots, ids = line[0:1, :], line[1:2, :]
    low = jnp.where(lanes // HALF == zh, pltpu.roll(slots, zh * HALF, 1), 0)
    high = jnp.where(lanes // HALF == NH + zh, pltpu.roll(slots, (NH - 1 + zh) * HALF, 1), 0)
    meta[c, x, zh, 0:1, :] = low + high
    meta[c, x, zh, 1:2, :] = jnp.where(lanes // ROWS == zh, pltpu.roll(ids, zh * ROWS, 1), 0)
    edge = pl.ds(WIDE - 128, 128)
    lt[:, edge] = jnp.full((TOK, 128), -jnp.inf, F32)
    lr[:, edge] = jnp.full((TOK, 128), -jnp.inf, F32)
    for cp in copies[2:7]:
        cp.wait()
    pl.semaphore_wait(barrier, len(near))

    right, left = dev(dz=1), dev(dz=-1)
    outward = tuple(zl * a + (1 - zl) * b for a, b in zip(right, left))
    inward = tuple(zl * b + (1 - zl) * a for a, b in zip(right, left))
    xr, xl = dev(dx=1), dev(dx=-1)
    yu, yd = dev(dy=1), dev(dy=-1)
    z_near, z_away = (1 - zl) * zm + zl * zp, (1 - zl) * zp + zl * zm
    zz = (zm, zp, zo)

    v_z = (1 - zl) * 4 + y
    v_up, v_dn, v_far = [zl * 4 + y_at[d] for d in (1, 3, 2)]
    w_up, w_dn, w_far = [(1 - zl) * 4 + y_at[d] for d in (1, 3, 2)]
    features = (v, v_z, v_dn, v_up, v_far, w_dn, w_up, w_far)

    block = {}

    def small(vv, xx, zq):
        return r.at[vv, c, xx, :, zq]

    for k in range(3):
        block["sz", k] = small(v, x, zz[k])
        block["sx", k] = small(v, (xm, xp, xo)[k], zh)
        block["mz", k] = meta.at[c, x, zz[k]]
        block["mx", k] = meta.at[c, (xm, xp, xo)[k]]
        block["s2l", k] = small(v, xm, zz[k])
        block["s2r", k] = small(v, xp, zz[k])
        block["s3l", k] = r.at[v, c, xo, 0, zz[k]]
        block["s3r", k] = r.at[v, c, xo, 1, zz[k]]
    block["ms", 0] = meta.at[1 - c]
    block["w", 0] = w.at[COLS:]
    order = [(x, zh)] + [(x, q) for q in zz] + [(xx, zh) for xx in xg[1:]] + [(xx, q) for xx in xg[1:] for q in zz]
    for k, (xx, zq) in enumerate(order):
        block["yu", k] = small(v_dn, xx, zq)
        block["yd", k] = small(v_up, xx, zq)
    for g in range(4):
        block["rr", g] = r.at[v_z, c, xg[g], 0]
        block["rl", g] = r.at[v_z, c, xg[g], 1]
        block["cu", g] = r.at[w_dn, c, xg[g]]
        block["cd", g] = r.at[w_up, c, xg[g]]
        block["fu", g] = r.at[v_far, c, xg[g], 1]
        block["fd", g] = r.at[v_far, c, xg[g], 0]
        block["lr", g] = r.at[w_far, c, xg[g], 0]
        block["ll", g] = r.at[w_far, c, xg[g], 1]
    for k in range(8):
        block["v", k] = r.at[features[k], 1 - c]

    def qn(k):
        return zl * (3 - k) + (1 - zl) * k

    def qf(k):
        return zl * k + (1 - zl) * (3 - k)

    def near_block(xx, k):
        return t.at[xx, z_near if k < 4 else zo, qn(k % 4)]

    def away_block(xx, k):
        return t.at[xx, z_away if k < 4 else zo, qf(k % 4)]

    quarter = {}
    for k in range(6):
        for g, xx in enumerate((x, xo)):
            block["tn%d" % g, k] = near_block(xx, k)
            block["tf%d" % g, k] = away_block(xx, k)
            quarter["tn%d" % g, k] = 3 - k % 4
            quarter["tf%d" % g, k] = k % 4
        for name, xx in (("tl", xm), ("tr", xp)):
            block[name, 4 + 2 * k] = near_block(xx, k)
            block[name, 5 + 2 * k] = away_block(xx, k)
            quarter[name, 4 + 2 * k] = 3 - k % 4
            quarter[name, 5 + 2 * k] = k % 4
    for k in range(4):
        block["tl", k] = t.at[xm, zh, qf(k)]
        block["tr", k] = t.at[xp, zh, qf((k + 2) % 4)]
        quarter["tl", k] = k
        quarter["tr", k] = (k + 2) % 4
    for k in range(2):
        block["ul", k] = t.at[xo, zh, qf(k)]
        block["ur", k] = t.at[xo, zh, qf(k + 2)]
        quarter["ul", k] = k
        quarter["ur", k] = k + 2
    def wait_key(name, k):
        if name in ("yu", "yd"):
            g = [n for n in range(4) if k in members[n]][0]
            return (name, g), r.at[v_dn if name == "yu" else v_up, c, xg[g]]
        if name in ("rr", "rl"):
            return ("rr", k), r.at[v_z, c, xg[k]]
        if name in ("fu", "fd"):
            return ("fu", k), r.at[v_far, c, xg[k]]
        if name in ("s3l", "s3r"):
            return ("s3l", k), small(v, xo, zz[k])
        if name in ("cu", "cd"):
            return (name, 0), r.at[w_dn if name == "cu" else w_up, c]
        if name in ("lr", "ll"):
            return ("lr", 0), r.at[w_far, c]
        if name == "mz":
            return (name, 0), meta.at[c, x, pl.ds(0, 3)]
        if name == "mx":
            return (name, 0), meta.at[c, pl.ds(0, 3)]
        if name in ("tl", "tr") and k >= 4:
            return ("tq", quarter[name, k]), t.at[0, pl.ds(0, 3), pl.ds(0, 2)]
        return (name, k), block[name, k]

    members = ((0, 1, 2, 3), (4, 7, 8, 9), (5, 10, 11, 12), (6, 13, 14, 15))
    wait_of = {name: wait_key(*name) for name in block}
    keys = {}
    for key, _ in wait_of.values():
        keys.setdefault(key, len(keys))
    assert len(keys) == ARRIVALS, len(keys)

    sent = {n: 0 for n in range(11)}
    waited = set()

    def send_sem(name):
        if name in ("v", "w"):
            n = 0 if name == "v" else 1
        elif name in ("rr", "rl", "cu", "cd", "fu", "fd", "lr", "ll"):
            n = 4
        elif name in ("s3l", "s3r"):
            n = 7
        elif name in ("mz", "mx", "ms"):
            n = 8 + ("mz", "mx", "ms").index(name)
        elif name in ("sz", "sx", "s2l", "s2r", "yu", "yd"):
            n = 5 if sent[5] < 32 else 6
        else:
            n = 2 if sent[2] < 48 else 3
        sent[n] += 1
        return n

    def put(name, n, ref, to, dst=None):
        pltpu.make_async_remote_copy(
            src_ref=ref, dst_ref=ref if dst is None else dst, send_sem=ssem.at[send_sem(name)],
            recv_sem=rsem.at[keys[wait_of[name, n][0]]], device_id=to, device_id_type=MESH).start()

    def all_sent():
        whole_sends = (
            r.at[:, 0], w.at[:COLS], t.at[pl.ds(0, 3)], t.at[0, pl.ds(0, 3)], r.at[pl.ds(0, 5), 0],
            r.at[:, 0, :, :, 0], r.at[pl.ds(0, 3), 0, :, :, 0], r.at[pl.ds(0, 3), 0, 0, :, 0],
            meta.at[0, 0, pl.ds(0, 3)], meta.at[0, pl.ds(0, 3)], meta.at[0],
        )
        assert tuple(sent.values()) == (8, 1, 48, 12, 32, 32, 12, 6, 3, 3, 1), sent
        for n, ref in enumerate(whole_sends):
            pltpu.make_async_remote_copy(
                src_ref=ref, dst_ref=ref, send_sem=ssem.at[n], recv_sem=ssem.at[n],
                device_id=partner, device_id_type=MESH).wait_send()

    def need(*names):
        for name in names:
            key, ref = wait_of[name]
            if key not in waited:
                waited.add(key)
                sem = rsem.at[keys[key]]
                pltpu.make_async_remote_copy(
                    src_ref=ref, dst_ref=ref, send_sem=sem, recv_sem=sem,
                    device_id=partner, device_id_type=MESH).wait_recv()

    def up_down(k, ref):
        put("yu", k, ref, yu)
        put("yd", k, ref, yd)

    own = small(v, x, zh)
    of_group = (
        [("sz", k) for k in range(3)],
        [("sx", 0)] + [("s2l", k) for k in range(3)],
        [("sx", 1)] + [("s2r", k) for k in range(3)],
        [("sx", 2)] + [(a, k) for a in ("s3l", "s3r") for k in range(3)],
    )
    whole = (
        sum(of_group, []),
        [(a, g) for a in ("rr", "rl") for g in range(4)],
        [("yu", k) for k in range(16)],
        [("yd", k) for k in range(16)],
        [(a, g) for a in ("fu", "fd") for g in range(4)],
        [("cu", g) for g in range(4)],
        [("cd", g) for g in range(4)],
        [(a, g) for a in ("lr", "ll") for g in range(4)],
    )

    def do(task, k):
        if task == "start":
            for n, d in enumerate((2, -2, 4)):
                put("sz", n, own, dev(dz=d))
            for n, d in enumerate((1, -1, 2)):
                put("sx", n, own, dev(dx=d))
            up_down(0, own)
            for n, d in enumerate((2, -2, 4)):
                put("mz", n, meta.at[c, x, zh], dev(dz=d))
        elif task == "head":
            copies[7].wait()
            put("w", 0, w.at[:COLS], partner, w.at[COLS:])
        elif task == "fx" and k < 4:
            put("tl", k, t.at[x, zh, qf(k)], xr)
            put("tr", k, t.at[x, zh, qf((k + 2) % 4)], xl)
        elif task == "fx":
            name = ("tf0", (k - 5) // 2) if k % 2 else ("tn0", (k - 4) // 2)
            need(name)
            put("tl", k, block[name], xr)
            put("tr", k, block[name], xl)
        elif task == "tzown":
            put("tn0", k, t.at[x, zh, qf(k)], outward)
        elif task == "meta1":
            need(("mz", 0), ("mz", 1), ("mz", 2))
            for n, d in enumerate((1, -1, 2)):
                put("mx", n, meta.at[c, x], dev(dx=d))
        elif task == "meta2":
            need(("mx", 0), ("mx", 1), ("mx", 2))
            put("ms", 0, meta.at[c], partner)
        elif task == "sz":
            need(("sz", k))
            ref = block["sz", k]
            put("s2l", k, ref, xr)
            put("s2r", k, ref, xl)
        elif task == "yz":
            need(("sz", k))
            up_down(1 + k, block["sz", k])
        elif task == "sx":
            need(("sx", k))
            up_down(4 + k, block["sx", k])
        elif task == "s2l":
            need(("s2l", k))
            put("s3l", k, r.at[v, c, xm, 0, zz[k]], xr)
        elif task == "y2l":
            need(("s2l", k))
            up_down(7 + k, block["s2l", k])
        elif task == "s2r":
            need(("s2r", k))
            put("s3r", k, r.at[v, c, xp, 1, zz[k]], xl)
        elif task == "y2r":
            need(("s2r", k))
            up_down(10 + k, block["s2r", k])
        elif task == "s3":
            need(("s3l", k), ("s3r", k))
            up_down(13 + k, small(v, xo, zz[k]))
        elif task == "spread":
            need(*of_group[k])
            put("rr", k, r.at[v, c, xg[k], 0], right)
            put("rl", k, r.at[v, c, xg[k], 1], left)
        elif task == "cross":
            need(("rr", k), ("rl", k))
            put("cu", k, r.at[v_z, c, xg[k]], yu)
            put("cd", k, r.at[v_z, c, xg[k]], yd)
        elif task == "relayu":
            need(*[("yu", i) for i in members[k]])
            put("fu", k, r.at[v_dn, c, xg[k], 1], yu)
        elif task == "relayd":
            need(*[("yd", i) for i in members[k]])
            put("fd", k, r.at[v_up, c, xg[k], 0], yd)
        elif task == "far":
            need(("fu", k), ("fd", k))
            put("lr", k, r.at[v_far, c, xg[k], 0], right)
            put("ll", k, r.at[v_far, c, xg[k], 1], left)
        elif task == "swap":
            need(*whole[k])
            put("v", k, r.at[features[k], c], partner)
        elif task in ("near0", "near1"):
            g = task[-1]
            need(("tn" + g, k))
            ref = block["tn" + g, k]
            put("tf" + g, k, ref, inward)
        elif task in ("away0", "away1"):
            g = task[-1]
            need(("tf" + g, k))
            put("tn" + g, 4 + k, block["tf" + g, k], outward)
        elif task == "tl":
            need(("tl", k))
            put("ul", k, block["tl", k], xr)
        elif task == "tr":
            need(("tr", k))
            put("ur", k, block["tr", k], xl)
        elif task == "own1":
            name = ("ul", k) if k < 2 else ("ur", k - 2)
            need(name)
            put("tn1", k, block[name], outward)
        elif task == "R":
            need(("v", k), ("w", 0), *whole[k])
            rollout_part(features[k])
        elif task == "T":
            need(("w", 0), *[name for name, q in quarter.items() if q == k])
            trainer_part(qf(k))
        elif task == "onehot":
            need(("ms", 0))
            fill_onehot()
        elif task == "TS":
            lax.fori_loop(0, NX, train_stats, 0)
        elif task == "RS":
            lax.fori_loop(0, NX, roll_stats, 0)

    def fill_onehot():
        place = lax.broadcasted_iota(jnp.int32, (TOK, GROUP), 0)
        for cc in range(2):
            for xx in range(NX):
                slot = meta[cc, xx, 0, 0:1, :]
                for zq in range(1, NH):
                    slot = slot + meta[cc, xx, zq, 0:1, :]
                token = (slot >> 6) * ROWS + (slot & (ROWS - 1))
                token = jnp.where(((slot >> 5) & 1) == c, token, -1)
                n = cc * NX + xx
                onehot[:, n * GROUP:(n + 1) * GROUP] = jnp.where(place == token, 1.0, 0.0).astype(BF16)

    def logits(rows, f):
        return lax.dot_general(rows, w[:, f], (((1,), (1,)), ((), ())), preferred_element_type=F32)

    begun = set()

    def add(logit, part):
        if id(logit) in begun:
            logit[:, :2 * COLS] += part
        else:
            begun.add(id(logit))
            logit[:, :2 * COLS] = part

    def rollout_part(vv):
        rows = r[vv].reshape(2 * TOK, FEAT)
        perm[...] = jnp.dot(onehot[...], rows, preferred_element_type=F32).astype(BF16)
        add(lr, logits(perm[...], pl.ds(pl.multiple_of(vv * FEAT, FEAT), FEAT)))

    def trainer_part(q):
        rows = t[:, :, pl.ds(q, 1)].reshape(TOK, PART)
        add(lt, logits(rows, pl.ds(pl.multiple_of(q * PART, PART), PART)))

    lane = lax.broadcasted_iota(jnp.int32, (GROUP, 128), 1)
    diagonal = lax.broadcasted_iota(jnp.int32, (GROUP, 128), 0) == lane

    def to_row(values):
        return jnp.sum(jnp.where(diagonal, values, 0), axis=0, keepdims=True)

    def to_column(values):
        return jnp.sum(jnp.where(diagonal, values, 0), axis=1, keepdims=True)

    def rows_of(xx):
        return pl.ds(pl.multiple_of(xx * GROUP, GROUP), GROUP)

    tiles = [pl.ds(128 * j, 128) for j in range(WIDE // 128)]

    def group_stats(logit, ex, stat, xx):
        rows = rows_of(xx)
        top = logit[rows, tiles[0]]
        for tile in tiles[1:]:
            top = jnp.maximum(top, logit[rows, tile])
        top = jnp.max(top, axis=1, keepdims=True)
        total = jnp.zeros((GROUP, 128), F32)
        for tile in tiles:
            e = jnp.exp(logit[rows, tile] - top)
            ex[rows, tile] = e
            total = total + e
        stat[xx, 0:1, :] = to_row(top)
        stat[xx, 1:2, :] = to_row(jnp.sum(total, axis=1, keepdims=True))

    def group_picks(logit, stat, xx):
        rows = rows_of(xx)
        ids = meta[c, xx, 0, 1:2, :]
        for zq in range(1, NH):
            ids = ids + meta[c, xx, zq, 1:2, :]
        ids = to_column(ids)
        pick = jnp.zeros((GROUP, 128), F32)
        for n, tile in enumerate(tiles):
            column = lanes + 128 * n
            column = jnp.where(
                column < COLS, column + (s * 8 + v) * COLS,
                jnp.where(column < 2 * COLS, column + ((s + 1 - 2 * c) * 8 + v) * COLS - COLS, -1))
            pick = pick + jnp.where(column == ids, logit[rows, tile], 0.0)
        stat[xx, 2:3, :] = to_row(jnp.sum(pick, axis=1, keepdims=True))

    def train_stats(xx, carry):
        group_stats(lt, et, stat_t, xx)
        group_picks(lt, stat_t, xx)
        return carry

    def roll_stats(xx, carry):
        group_stats(lr, er, stat_r, xx)
        return carry

    def roll_picks(xx, carry):
        group_picks(lr, stat_r, xx)
        return carry

    def exchange(buf, sem, away):
        count = len(away) + 1
        for n, offset in enumerate(away):
            pltpu.make_async_remote_copy(
                src_ref=buf.at[0], dst_ref=buf.at[n + 1], send_sem=a_sem.at[sem], recv_sem=a_sem.at[sem + 1],
                device_id=dev(*offset), device_id_type=MESH).start()
        rest = buf.at[pl.ds(1, count - 1)]
        return pltpu.make_async_remote_copy(
            src_ref=rest, dst_ref=rest, send_sem=a_sem.at[sem], recv_sem=a_sem.at[sem + 1],
            device_id=partner, device_id_type=MESH)

    def merge(buf, count):
        top = buf[0, 0]
        for d in range(1, count):
            top = jnp.maximum(top, buf[d, 0])
        total = jnp.zeros_like(top)
        for d in range(count):
            total = total + buf[d, 1] * jnp.exp(buf[d, 0] - top)
        return top, total

    def plane(n, stat):
        a1[n, 0, 0] = stat[:, 0, :]
        a1[n, 0, 1] = stat[:, 1, :]
        return exchange(a1.at[n], 4 * n, offsets(NX, NY, 1))

    def column_z(n, before):
        before.wait_recv()
        top, total = merge(a1.at[n], 16)
        a2[n, 0, 0] = top
        a2[n, 0, 1] = total
        return exchange(a2.at[n], 4 * n + 2, offsets(1, 1, NZ))

    def finish(n, before):
        before.wait_recv()
        top, total = merge(a2.at[n], 8)
        fin[n, 0] = top
        fin[n, 1] = total

    for task, k in ORDER:
        do(task, k)
        if task == "TS":
            plane_t = plane(1, stat_t)
    plane_r = plane(0, stat_r)
    column_t = column_z(1, plane_t)
    lax.fori_loop(0, NX, roll_picks, 0)
    column_r = column_z(0, plane_r)
    finish(1, column_t)
    finish(0, column_r)

    def compare(xx, carry):
        rows = pl.ds(pl.multiple_of(xx * GROUP, GROUP), GROUP)
        scale_r = jnp.exp(stat_r[xx, 0:1, :] - fin[0, 0, pl.ds(xx, 1), :]) / fin[0, 1, pl.ds(xx, 1), :]
        scale_t = jnp.exp(stat_t[xx, 0:1, :] - fin[1, 0, pl.ds(xx, 1), :]) / fin[1, 1, pl.ds(xx, 1), :]
        scale_r, scale_t = to_column(scale_r), to_column(scale_t)
        shared = jnp.zeros((GROUP, 128), F32)
        squares = jnp.zeros((GROUP, 128), F32)
        for tile in tiles:
            p = er[rows, tile] * scale_r
            q = et[rows, tile] * scale_t
            shared = shared + jnp.minimum(p, q)
            squares = squares + (q - p) * (q - p)
        shared = to_row(jnp.sum(shared, axis=1, keepdims=True))
        squares = to_row(jnp.sum(squares, axis=1, keepdims=True))
        values = (shared, squares, stat_r[xx, 2:3, :], stat_t[xx, 2:3, :])
        part = lax.broadcasted_iota(jnp.int32, (1, 128), 1) // ROWS
        for zq in range(NH):
            one = jnp.zeros((1, 128), F32)
            for k in range(4):
                one = one + jnp.where(part == k, pltpu.roll(values[k], ((k - zq) % 4) * ROWS, 1), 0.0)
            out2[xx, zq] = one
        return carry
    lax.fori_loop(0, NX, compare, 0)

    a3[0] = out2[x, zh]

    for n, (dx, dy, dz) in enumerate(offsets(NX, NY, NZ)):
        pltpu.make_async_remote_copy(
            src_ref=out2.at[x_at[dx], zh_at[dz]], dst_ref=a3.at[n + 1], send_sem=a_sem.at[8], recv_sem=a_sem.at[9],
            device_id=dev(dx, dy, dz), device_id_type=MESH).start()
    rest = a3.at[pl.ds(1, 127)]
    done3 = pltpu.make_async_remote_copy(
        src_ref=rest, dst_ref=rest, send_sem=a_sem.at[8], recv_sem=a_sem.at[9],
        device_id=partner, device_id_type=MESH)
    all_sent()
    for done in (plane_t, plane_r, column_t, column_r):
        done.wait_send()
    done3.wait_recv()
    sums = jnp.sum(a3[...], axis=0)
    shift = (NH - zh) % NH * ROWS
    own_top = [pltpu.roll(fin[n, 0, pl.ds(x, 1), :], shift, 1)[:, :ROWS] for n in range(2)]
    own_total = [pltpu.roll(fin[n, 1, pl.ds(x, 1), :], shift, 1)[:, :ROWS] for n in range(2)]
    pick_r = pltpu.roll(sums, 2 * ROWS, 1)[:, :ROWS]
    pick_t = pltpu.roll(sums, ROWS, 1)[:, :ROWS]
    squares = pltpu.roll(sums, 3 * ROWS, 1)[:, :ROWS]
    log_ratio = pick_t - own_top[1] - jnp.log(own_total[1]) - (pick_r - own_top[0] - jnp.log(own_total[0]))
    out[0:1, :] = sums[:, :ROWS]
    out[1:2, :] = jnp.sqrt(squares + 1e-06)
    out[2:3, :] = jnp.minimum(jnp.exp(log_ratio), 2.0)
    done3.wait_send()


def per_device(rollout_hidden, trainer_hidden, head_weight, token_ids, response_mask, trainer_slot):
    dma, reg = pltpu.SemaphoreType.DMA, pl.BlockSpec(memory_space=pl.ANY)
    vmem = pl.BlockSpec(memory_space=pltpu.VMEM)
    sums = pl.pallas_call(
        kernel,
        out_shape=jax.ShapeDtypeStruct((3, ROWS), F32),
        in_specs=[reg] * 5,
        out_specs=vmem,
        scratch_shapes=[
            pltpu.VMEM((2 * COLS, D), BF16),
            pltpu.VMEM((NX, NH, 4, ROWS, PART), BF16),
            pltpu.VMEM((8, 2, NX, 2, NH, HALF, FEAT), BF16),
            pltpu.VMEM((1, ROWS), jnp.int32),
            pltpu.VMEM((1, ROWS), jnp.int32),
            pltpu.VMEM((2, 128), jnp.int32),
            pltpu.VMEM((2, NX, NH, 2, 128), jnp.int32),
            pltpu.VMEM((TOK, 2 * TOK), BF16),
            pltpu.VMEM((TOK, FEAT), BF16),
            pltpu.VMEM((TOK, WIDE), F32),
            pltpu.VMEM((TOK, WIDE), F32),
            pltpu.VMEM((TOK, WIDE), F32),
            pltpu.VMEM((TOK, WIDE), F32),
            pltpu.VMEM((NX, 8, 128), F32),
            pltpu.VMEM((NX, 8, 128), F32),
            pltpu.VMEM((2, 16, 2, NX, 128), F32),
            pltpu.VMEM((2, 8, 2, NX, 128), F32),
            pltpu.VMEM((2, 2, NX, 128), F32),
            pltpu.VMEM((NX, NH, 1, 128), F32),
            pltpu.VMEM((128, 1, 128), F32),
            dma((11,)), dma((ARRIVALS,)), dma((8,)), dma((10,)),
        ],
        compiler_params=pltpu.CompilerParams(
            collective_id=0, has_side_effects=True, vmem_limit_bytes=60 * 1024 * 1024),
        cost_estimate=pl.CostEstimate(
            flops=2 * 2 * TOK * D * 2 * COLS + 2 * TOK * 2 * TOK * D, bytes_accessed=D * COLS * 2, transcendentals=2 * TOK * 2 * COLS),
    )(rollout_hidden.reshape(2, HALF, FEAT), trainer_hidden, head_weight.T,
      trainer_slot.reshape(1, ROWS), token_ids.reshape(1, ROWS))
    mask = response_mask.astype(F32)
    return tuple(sums[n] * mask for n in range(3))


def solution(mesh):
    placed = (
        P("seq", "vocab"),
        P("seq", None),
        P(None, ("seq", "vocab")),
        P("seq"),
        P("seq"),
        P("seq"),
    )
    return jax.shard_map(
        per_device,
        mesh=mesh,
        in_specs=placed,
        out_specs=(P("seq"), P("seq"), P("seq")),
        check_vma=False,
    )
```

```python
import jax
import jax.numpy as jnp
from jax import lax
from jax.experimental import pallas as pl
from jax.experimental.pallas import tpu as pltpu
from jax.sharding import PartitionSpec as P

MESH = pl.DeviceIdType.MESH
BF16 = jnp.bfloat16
F32 = jnp.float32
NX, NY, NZ, NH = 4, 4, 8, 4
ROWS = 32
HALF = 16
D = 4096
FEAT = 512
COLS = 592
WIDE = 1280
TOK = 512
GROUP = 128
PART = 1024
ARRIVALS = 86

ORDER = (
    ("fx", 0), ("start", 0), ("fx", 1), ("tzown", 0), ("fx", 3), ("tzown", 2),
    ("tl", 0), ("tr", 0), ("tzown", 1), ("sx", 0), ("yz", 0), ("head", 0),
    ("yz", 1), ("sx", 1), ("sz", 0), ("tzown", 3), ("sx", 2), ("sz", 1),
    ("near0", 0), ("tl", 1), ("tr", 1), ("spread", 0), ("yz", 2), ("near0", 2),
    ("meta1", 0), ("fx", 4), ("own1", 0), ("near0", 1), ("sz", 2), ("own1", 2),
    ("y2l", 0), ("y2r", 0), ("s2r", 0), ("s2l", 0), ("fx", 5), ("y2r", 1),
    ("near0", 3), ("y2l", 1), ("away0", 0), ("relayu", 0), ("relayd", 0), ("s2r", 1),
    ("s2l", 1), ("fx", 6), ("own1", 3), ("cross", 0), ("meta2", 0), ("near1", 0),
    ("fx", 9), ("own1", 1), ("onehot", 0), ("near1", 2), ("s2r", 2), ("s2l", 2),
    ("spread", 2), ("y2r", 2), ("fx", 7), ("s3", 0), ("near0", 4), ("away0", 1),
    ("y2l", 2), ("fx", 11), ("s3", 1), ("near1", 3), ("away1", 0), ("fx", 12),
    ("near1", 1), ("swap", 0), ("s3", 2), ("fx", 10), ("relayu", 2), ("relayd", 2),
    ("spread", 1), ("cross", 2), ("fx", 2), ("R", 0), ("swap", 2), ("relayu", 1),
    ("relayd", 1), ("fx", 13), ("spread", 3), ("near1", 4), ("swap", 3), ("T", 3),
    ("relayu", 3), ("near0", 5), ("relayd", 3), ("away1", 1), ("fx", 14), ("fx", 8),
    ("R", 2), ("far", 2), ("cross", 1), ("swap", 1), ("R", 3), ("far", 0),
    ("cross", 3), ("far", 1), ("T", 0), ("near1", 5), ("fx", 15), ("swap", 4),
    ("T", 2), ("far", 3), ("R", 1), ("R", 4), ("swap", 5), ("swap", 6),
    ("T", 1), ("TS", 0), ("swap", 7), ("R", 5), ("R", 6), ("R", 7),
    ("RS", 0),
)


def kernel(roll_in, train_in, head_in, slot_in, ids_in, out,
           w, t, r, slot_v, ids_v, line, meta, onehot, perm, lt, lr, et, er, stat_r, stat_t, a1, a2, fin, out2, a3,
           ssem, rsem, in_sem, a_sem):
    s, v = lax.axis_index("seq"), lax.axis_index("vocab")
    x, zh, c = lax.div(s, 8), lax.rem(lax.div(s, 2), 4), lax.rem(s, 2)
    zl, y = lax.div(v, 4), lax.rem(v, 4)
    z = zh * 2 + zl

    x_at = [lax.rem(x + d, NX) for d in range(NX)]
    y_at = [lax.rem(y + d, NY) for d in range(NY)]
    z_at = [lax.rem(z + d, NZ) for d in range(NZ)]
    zh_at = [lax.div(zz, 2) for zz in z_at]
    seq_x = [8 * xx + c for xx in x_at]
    seq_z = [2 * zz for zz in zh_at]
    vocab_z = [4 * lax.rem(zz, 2) for zz in z_at]

    def dev(dx=0, dy=0, dz=0):
        return (seq_x[dx % NX] + seq_z[dz % NZ], vocab_z[dz % NZ] + y_at[dy % NY])

    def offsets(xs, ys, zs):
        every = [(dx, dy, dz) for dx in range(xs) for dy in range(ys) for dz in range(zs)][1:]
        return sorted(every, key=lambda o: -min(o[0], NX - o[0]) - min(o[1], NY - o[1]) - min(o[2], NZ - o[2]))

    partner = (s + 1 - 2 * c, v)
    xm, xp, xo = x_at[3], x_at[1], x_at[2]
    xg = (x, xm, xp, xo)
    zm, zp, zo = zh_at[6], zh_at[2], zh_at[4]

    barrier = pltpu.get_barrier_semaphore()
    near = [dev(dz=d) for d in (4, 2, -2)] + [dev(dx=2)] + [dev(dx=d) for d in (1, -1)]
    near += [dev(dy=d) for d in (1, -1)] + [dev(dz=d) for d in (1, -1)] + [partner]
    for to in near:
        pl.semaphore_signal(barrier, inc=1, device_id=to, device_id_type=MESH)

    copies = [
        pltpu.make_async_copy(slot_in, slot_v, in_sem.at[6]),
        pltpu.make_async_copy(ids_in, ids_v, in_sem.at[7]),
        pltpu.make_async_copy(roll_in, r.at[v, c, x, :, zh], in_sem.at[0]),
    ]
    for q in range(4):
        copies.append(pltpu.make_async_copy(train_in.at[:, q * PART:(q + 1) * PART], t.at[x, zh, q], in_sem.at[1 + q]))
    copies.append(pltpu.make_async_copy(head_in, w.at[:COLS], in_sem.at[5]))
    for cp in copies:
        cp.start()
    for cp in copies[:2]:
        cp.wait()
    lanes = lax.broadcasted_iota(jnp.int32, (1, 128), 1)
    line[0:1, :ROWS] = slot_v[...]
    line[1:2, :ROWS] = ids_v[...]
    slots, ids = line[0:1, :], line[1:2, :]
    low = jnp.where(lanes // HALF == zh, pltpu.roll(slots, zh * HALF, 1), 0)
    high = jnp.where(lanes // HALF == NH + zh, pltpu.roll(slots, (NH - 1 + zh) * HALF, 1), 0)
    meta[c, x, zh, 0:1, :] = low + high
    meta[c, x, zh, 1:2, :] = jnp.where(lanes // ROWS == zh, pltpu.roll(ids, zh * ROWS, 1), 0)
    edge = pl.ds(WIDE - 128, 128)
    lt[:, edge] = jnp.full((TOK, 128), -jnp.inf, F32)
    lr[:, edge] = jnp.full((TOK, 128), -jnp.inf, F32)
    for cp in copies[2:7]:
        cp.wait()
    pl.semaphore_wait(barrier, len(near))

    right, left = dev(dz=1), dev(dz=-1)
    outward = tuple(zl * a + (1 - zl) * b for a, b in zip(right, left))
    inward = tuple(zl * b + (1 - zl) * a for a, b in zip(right, left))
    xr, xl = dev(dx=1), dev(dx=-1)
    yu, yd = dev(dy=1), dev(dy=-1)
    z_near, z_away = (1 - zl) * zm + zl * zp, (1 - zl) * zp + zl * zm
    zz = (zm, zp, zo)

    v_z = (1 - zl) * 4 + y
    v_up, v_dn, v_far = [zl * 4 + y_at[d] for d in (1, 3, 2)]
    w_up, w_dn, w_far = [(1 - zl) * 4 + y_at[d] for d in (1, 3, 2)]
    features = (v, v_z, v_dn, v_up, v_far, w_dn, w_up, w_far)

    block = {}

    def small(vv, xx, zq):
        return r.at[vv, c, xx, :, zq]

    for k in range(3):
        block["sz", k] = small(v, x, zz[k])
        block["sx", k] = small(v, (xm, xp, xo)[k], zh)
        block["mz", k] = meta.at[c, x, zz[k]]
        block["mx", k] = meta.at[c, (xm, xp, xo)[k]]
        block["s2l", k] = small(v, xm, zz[k])
        block["s2r", k] = small(v, xp, zz[k])
        block["s3l", k] = r.at[v, c, xo, 0, zz[k]]
        block["s3r", k] = r.at[v, c, xo, 1, zz[k]]
    block["ms", 0] = meta.at[1 - c]
    block["w", 0] = w.at[COLS:]
    order = [(x, zh)] + [(x, q) for q in zz] + [(xx, zh) for xx in xg[1:]] + [(xx, q) for xx in xg[1:] for q in zz]
    for k, (xx, zq) in enumerate(order):
        block["yu", k] = small(v_dn, xx, zq)
        block["yd", k] = small(v_up, xx, zq)
    for g in range(4):
        block["rr", g] = r.at[v_z, c, xg[g], 0]
        block["rl", g] = r.at[v_z, c, xg[g], 1]
        block["cu", g] = r.at[w_dn, c, xg[g]]
        block["cd", g] = r.at[w_up, c, xg[g]]
        block["fu", g] = r.at[v_far, c, xg[g], 1]
        block["fd", g] = r.at[v_far, c, xg[g], 0]
        block["lr", g] = r.at[w_far, c, xg[g], 0]
        block["ll", g] = r.at[w_far, c, xg[g], 1]
    for k in range(8):
        block["v", k] = r.at[features[k], 1 - c]

    def qn(k):
        return zl * (3 - k) + (1 - zl) * k

    def qf(k):
        return zl * k + (1 - zl) * (3 - k)

    def near_block(xx, k):
        return t.at[xx, z_near if k < 4 else zo, qn(k % 4)]

    def away_block(xx, k):
        return t.at[xx, z_away if k < 4 else zo, qf(k % 4)]

    quarter = {}
    for k in range(6):
        for g, xx in enumerate((x, xo)):
            block["tn%d" % g, k] = near_block(xx, k)
            block["tf%d" % g, k] = away_block(xx, k)
            quarter["tn%d" % g, k] = 3 - k % 4
            quarter["tf%d" % g, k] = k % 4
        for name, xx in (("tl", xm), ("tr", xp)):
            block[name, 4 + 2 * k] = near_block(xx, k)
            block[name, 5 + 2 * k] = away_block(xx, k)
            quarter[name, 4 + 2 * k] = 3 - k % 4
            quarter[name, 5 + 2 * k] = k % 4
    for k in range(4):
        block["tl", k] = t.at[xm, zh, qf(k)]
        block["tr", k] = t.at[xp, zh, qf((k + 2) % 4)]
        quarter["tl", k] = k
        quarter["tr", k] = (k + 2) % 4
    for k in range(2):
        block["ul", k] = t.at[xo, zh, qf(k)]
        block["ur", k] = t.at[xo, zh, qf(k + 2)]
        quarter["ul", k] = k
        quarter["ur", k] = k + 2
    def wait_key(name, k):
        if name in ("yu", "yd"):
            g = [n for n in range(4) if k in members[n]][0]
            return (name, g), r.at[v_dn if name == "yu" else v_up, c, xg[g]]
        if name in ("rr", "rl"):
            return ("rr", k), r.at[v_z, c, xg[k]]
        if name in ("fu", "fd"):
            return ("fu", k), r.at[v_far, c, xg[k]]
        if name in ("s3l", "s3r"):
            return ("s3l", k), small(v, xo, zz[k])
        if name in ("cu", "cd"):
            return (name, 0), r.at[w_dn if name == "cu" else w_up, c]
        if name in ("lr", "ll"):
            return ("lr", 0), r.at[w_far, c]
        if name == "mz":
            return (name, 0), meta.at[c, x, pl.ds(0, 3)]
        if name == "mx":
            return (name, 0), meta.at[c, pl.ds(0, 3)]
        if name in ("tl", "tr") and k >= 4:
            return ("tq", quarter[name, k]), t.at[0, pl.ds(0, 3), pl.ds(0, 2)]
        return (name, k), block[name, k]

    members = ((0, 1, 2, 3), (4, 7, 8, 9), (5, 10, 11, 12), (6, 13, 14, 15))
    wait_of = {name: wait_key(*name) for name in block}
    keys = {}
    for key, _ in wait_of.values():
        keys.setdefault(key, len(keys))
    assert len(keys) == ARRIVALS, len(keys)

    sent = {n: 0 for n in range(11)}
    waited = set()

    def send_sem(name):
        if name in ("v", "w"):
            n = 0 if name == "v" else 1
        elif name in ("rr", "rl", "cu", "cd", "fu", "fd", "lr", "ll"):
            n = 4
        elif name in ("s3l", "s3r"):
            n = 7
        elif name in ("mz", "mx", "ms"):
            n = 8 + ("mz", "mx", "ms").index(name)
        elif name in ("sz", "sx", "s2l", "s2r", "yu", "yd"):
            n = 5 if sent[5] < 32 else 6
        else:
            n = 2 if sent[2] < 48 else 3
        sent[n] += 1
        return n

    def put(name, n, ref, to, dst=None):
        pltpu.make_async_remote_copy(
            src_ref=ref, dst_ref=ref if dst is None else dst, send_sem=ssem.at[send_sem(name)],
            recv_sem=rsem.at[keys[wait_of[name, n][0]]], device_id=to, device_id_type=MESH).start()

    def all_sent():
        whole_sends = (
            r.at[:, 0], w.at[:COLS], t.at[pl.ds(0, 3)], t.at[0, pl.ds(0, 3)], r.at[pl.ds(0, 5), 0],
            r.at[:, 0, :, :, 0], r.at[pl.ds(0, 3), 0, :, :, 0], r.at[pl.ds(0, 3), 0, 0, :, 0],
            meta.at[0, 0, pl.ds(0, 3)], meta.at[0, pl.ds(0, 3)], meta.at[0],
        )
        assert tuple(sent.values()) == (8, 1, 48, 12, 32, 32, 12, 6, 3, 3, 1), sent
        for n, ref in enumerate(whole_sends):
            pltpu.make_async_remote_copy(
                src_ref=ref, dst_ref=ref, send_sem=ssem.at[n], recv_sem=ssem.at[n],
                device_id=partner, device_id_type=MESH).wait_send()

    def need(*names):
        for name in names:
            key, ref = wait_of[name]
            if key not in waited:
                waited.add(key)
                sem = rsem.at[keys[key]]
                pltpu.make_async_remote_copy(
                    src_ref=ref, dst_ref=ref, send_sem=sem, recv_sem=sem,
                    device_id=partner, device_id_type=MESH).wait_recv()

    def up_down(k, ref):
        put("yu", k, ref, yu)
        put("yd", k, ref, yd)

    own = small(v, x, zh)
    of_group = (
        [("sz", k) for k in range(3)],
        [("sx", 0)] + [("s2l", k) for k in range(3)],
        [("sx", 1)] + [("s2r", k) for k in range(3)],
        [("sx", 2)] + [(a, k) for a in ("s3l", "s3r") for k in range(3)],
    )
    whole = (
        sum(of_group, []),
        [(a, g) for a in ("rr", "rl") for g in range(4)],
        [("yu", k) for k in range(16)],
        [("yd", k) for k in range(16)],
        [(a, g) for a in ("fu", "fd") for g in range(4)],
        [("cu", g) for g in range(4)],
        [("cd", g) for g in range(4)],
        [(a, g) for a in ("lr", "ll") for g in range(4)],
    )

    def do(task, k):
        if task == "start":
            for n, d in enumerate((2, -2, 4)):
                put("sz", n, own, dev(dz=d))
            for n, d in enumerate((1, -1, 2)):
                put("sx", n, own, dev(dx=d))
            up_down(0, own)
            for n, d in enumerate((2, -2, 4)):
                put("mz", n, meta.at[c, x, zh], dev(dz=d))
        elif task == "head":
            copies[7].wait()
            put("w", 0, w.at[:COLS], partner, w.at[COLS:])
        elif task == "fx" and k < 4:
            put("tl", k, t.at[x, zh, qf(k)], xr)
            put("tr", k, t.at[x, zh, qf((k + 2) % 4)], xl)
        elif task == "fx":
            name = ("tf0", (k - 5) // 2) if k % 2 else ("tn0", (k - 4) // 2)
            need(name)
            put("tl", k, block[name], xr)
            put("tr", k, block[name], xl)
        elif task == "tzown":
            put("tn0", k, t.at[x, zh, qf(k)], outward)
        elif task == "meta1":
            need(("mz", 0), ("mz", 1), ("mz", 2))
            for n, d in enumerate((1, -1, 2)):
                put("mx", n, meta.at[c, x], dev(dx=d))
        elif task == "meta2":
            need(("mx", 0), ("mx", 1), ("mx", 2))
            put("ms", 0, meta.at[c], partner)
        elif task == "sz":
            need(("sz", k))
            ref = block["sz", k]
            put("s2l", k, ref, xr)
            put("s2r", k, ref, xl)
        elif task == "yz":
            need(("sz", k))
            up_down(1 + k, block["sz", k])
        elif task == "sx":
            need(("sx", k))
            up_down(4 + k, block["sx", k])
        elif task == "s2l":
            need(("s2l", k))
            put("s3l", k, r.at[v, c, xm, 0, zz[k]], xr)
        elif task == "y2l":
            need(("s2l", k))
            up_down(7 + k, block["s2l", k])
        elif task == "s2r":
            need(("s2r", k))
            put("s3r", k, r.at[v, c, xp, 1, zz[k]], xl)
        elif task == "y2r":
            need(("s2r", k))
            up_down(10 + k, block["s2r", k])
        elif task == "s3":
            need(("s3l", k), ("s3r", k))
            up_down(13 + k, small(v, xo, zz[k]))
        elif task == "spread":
            need(*of_group[k])
            put("rr", k, r.at[v, c, xg[k], 0], right)
            put("rl", k, r.at[v, c, xg[k], 1], left)
        elif task == "cross":
            need(("rr", k), ("rl", k))
            put("cu", k, r.at[v_z, c, xg[k]], yu)
            put("cd", k, r.at[v_z, c, xg[k]], yd)
        elif task == "relayu":
            need(*[("yu", i) for i in members[k]])
            put("fu", k, r.at[v_dn, c, xg[k], 1], yu)
        elif task == "relayd":
            need(*[("yd", i) for i in members[k]])
            put("fd", k, r.at[v_up, c, xg[k], 0], yd)
        elif task == "far":
            need(("fu", k), ("fd", k))
            put("lr", k, r.at[v_far, c, xg[k], 0], right)
            put("ll", k, r.at[v_far, c, xg[k], 1], left)
        elif task == "swap":
            need(*whole[k])
            put("v", k, r.at[features[k], c], partner)
        elif task in ("near0", "near1"):
            g = task[-1]
            need(("tn" + g, k))
            ref = block["tn" + g, k]
            put("tf" + g, k, ref, inward)
        elif task in ("away0", "away1"):
            g = task[-1]
            need(("tf" + g, k))
            put("tn" + g, 4 + k, block["tf" + g, k], outward)
        elif task == "tl":
            need(("tl", k))
            put("ul", k, block["tl", k], xr)
        elif task == "tr":
            need(("tr", k))
            put("ur", k, block["tr", k], xl)
        elif task == "own1":
            name = ("ul", k) if k < 2 else ("ur", k - 2)
            need(name)
            put("tn1", k, block[name], outward)
        elif task == "R":
            need(("v", k), ("w", 0), *whole[k])
            rollout_part(features[k])
        elif task == "T":
            need(("w", 0), *[name for name, q in quarter.items() if q == k])
            trainer_part(qf(k))
        elif task == "onehot":
            need(("ms", 0))
            fill_onehot()
        elif task == "TS":
            for xx in range(NX):
                train_stats(xx, 0)
        elif task == "RS":
            for xx in range(NX):
                roll_stats(xx, 0)

    def fill_onehot():
        place = lax.broadcasted_iota(jnp.int32, (TOK, GROUP), 0)
        for cc in range(2):
            for xx in range(NX):
                slot = meta[cc, xx, 0, 0:1, :]
                for zq in range(1, NH):
                    slot = slot + meta[cc, xx, zq, 0:1, :]
                token = (slot >> 6) * ROWS + (slot & (ROWS - 1))
                token = jnp.where(((slot >> 5) & 1) == c, token, -1)
                n = cc * NX + xx
                onehot[:, n * GROUP:(n + 1) * GROUP] = jnp.where(place == token, 1.0, 0.0).astype(BF16)

    def logits(rows, f):
        return lax.dot_general(rows, w[:, f], (((1,), (1,)), ((), ())), preferred_element_type=F32)

    begun = set()

    def add(logit, part):
        if id(logit) in begun:
            logit[:, :2 * COLS] += part
        else:
            begun.add(id(logit))
            logit[:, :2 * COLS] = part

    def rollout_part(vv):
        rows = r[vv].reshape(2 * TOK, FEAT)
        perm[...] = jnp.dot(onehot[...], rows, preferred_element_type=F32).astype(BF16)
        add(lr, logits(perm[...], pl.ds(pl.multiple_of(vv * FEAT, FEAT), FEAT)))

    def trainer_part(q):
        rows = t[:, :, pl.ds(q, 1)].reshape(TOK, PART)
        add(lt, logits(rows, pl.ds(pl.multiple_of(q * PART, PART), PART)))

    lane = lax.broadcasted_iota(jnp.int32, (GROUP, 128), 1)
    diagonal = lax.broadcasted_iota(jnp.int32, (GROUP, 128), 0) == lane

    def to_row(values):
        return jnp.sum(jnp.where(diagonal, values, 0), axis=0, keepdims=True)

    def to_column(values):
        return jnp.sum(jnp.where(diagonal, values, 0), axis=1, keepdims=True)

    def rows_of(xx):
        if isinstance(xx, int):
            return pl.ds(xx * GROUP, GROUP)
        return pl.ds(pl.multiple_of(xx * GROUP, GROUP), GROUP)

    tiles = [pl.ds(128 * j, 128) for j in range(WIDE // 128)]

    def group_stats(logit, ex, stat, xx):
        rows = rows_of(xx)
        top = logit[rows, tiles[0]]
        for tile in tiles[1:]:
            top = jnp.maximum(top, logit[rows, tile])
        top = jnp.max(top, axis=1, keepdims=True)
        total = jnp.zeros((GROUP, 128), F32)
        for tile in tiles:
            e = jnp.exp(logit[rows, tile] - top)
            ex[rows, tile] = e
            total = total + e
        stat[xx, 0:1, :] = to_row(top)
        stat[xx, 1:2, :] = to_row(jnp.sum(total, axis=1, keepdims=True))

    def group_picks(logit, stat, xx):
        rows = rows_of(xx)
        ids = meta[c, xx, 0, 1:2, :]
        for zq in range(1, NH):
            ids = ids + meta[c, xx, zq, 1:2, :]
        ids = to_column(ids)
        pick = jnp.zeros((GROUP, 128), F32)
        for n, tile in enumerate(tiles):
            column = lanes + 128 * n
            column = jnp.where(
                column < COLS, column + (s * 8 + v) * COLS,
                jnp.where(column < 2 * COLS, column + ((s + 1 - 2 * c) * 8 + v) * COLS - COLS, -1))
            pick = pick + jnp.where(column == ids, logit[rows, tile], 0.0)
        stat[xx, 2:3, :] = to_row(jnp.sum(pick, axis=1, keepdims=True))

    def train_stats(xx, carry):
        group_stats(lt, et, stat_t, xx)
        group_picks(lt, stat_t, xx)
        return carry

    def roll_stats(xx, carry):
        group_stats(lr, er, stat_r, xx)
        return carry

    def roll_picks(xx, carry):
        group_picks(lr, stat_r, xx)
        return carry

    def exchange(buf, sem, away):
        count = len(away) + 1
        for n, offset in enumerate(away):
            pltpu.make_async_remote_copy(
                src_ref=buf.at[0], dst_ref=buf.at[n + 1], send_sem=a_sem.at[sem], recv_sem=a_sem.at[sem + 1],
                device_id=dev(*offset), device_id_type=MESH).start()
        rest = buf.at[pl.ds(1, count - 1)]
        return pltpu.make_async_remote_copy(
            src_ref=rest, dst_ref=rest, send_sem=a_sem.at[sem], recv_sem=a_sem.at[sem + 1],
            device_id=partner, device_id_type=MESH)

    def merge(buf, count):
        top = buf[0, 0]
        for d in range(1, count):
            top = jnp.maximum(top, buf[d, 0])
        total = jnp.zeros_like(top)
        for d in range(count):
            total = total + buf[d, 1] * jnp.exp(buf[d, 0] - top)
        return top, total

    def plane(n, stat):
        a1[n, 0, 0] = stat[:, 0, :]
        a1[n, 0, 1] = stat[:, 1, :]
        return exchange(a1.at[n], 4 * n, offsets(NX, NY, 1))

    def column_z(n, before):
        before.wait_recv()
        top, total = merge(a1.at[n], 16)
        a2[n, 0, 0] = top
        a2[n, 0, 1] = total
        return exchange(a2.at[n], 4 * n + 2, offsets(1, 1, NZ))

    def finish(n, before):
        before.wait_recv()
        top, total = merge(a2.at[n], 8)
        fin[n, 0] = top
        fin[n, 1] = total

    for task, k in ORDER:
        do(task, k)
        if task == "TS":
            plane_t = plane(1, stat_t)
    plane_r = plane(0, stat_r)
    column_t = column_z(1, plane_t)
    lax.fori_loop(0, NX, roll_picks, 0)
    column_r = column_z(0, plane_r)
    finish(1, column_t)
    finish(0, column_r)

    def compare(xx, carry):
        rows = rows_of(xx)
        scale_r = jnp.exp(stat_r[xx, 0:1, :] - fin[0, 0, pl.ds(xx, 1), :]) / fin[0, 1, pl.ds(xx, 1), :]
        scale_t = jnp.exp(stat_t[xx, 0:1, :] - fin[1, 0, pl.ds(xx, 1), :]) / fin[1, 1, pl.ds(xx, 1), :]
        scale_r, scale_t = to_column(scale_r), to_column(scale_t)
        shared = jnp.zeros((GROUP, 128), F32)
        squares = jnp.zeros((GROUP, 128), F32)
        for tile in tiles:
            p = er[rows, tile] * scale_r
            q = et[rows, tile] * scale_t
            shared = shared + jnp.minimum(p, q)
            squares = squares + (q - p) * (q - p)
        shared = to_row(jnp.sum(shared, axis=1, keepdims=True))
        squares = to_row(jnp.sum(squares, axis=1, keepdims=True))
        values = (shared, squares, stat_r[xx, 2:3, :], stat_t[xx, 2:3, :])
        part = lax.broadcasted_iota(jnp.int32, (1, 128), 1) // ROWS
        for zq in range(NH):
            one = jnp.zeros((1, 128), F32)
            for k in range(4):
                one = one + jnp.where(part == k, pltpu.roll(values[k], ((k - zq) % 4) * ROWS, 1), 0.0)
            out2[xx, zq] = one
        return carry
    for xx in range(NX):
        compare(xx, 0)

    a3[0] = out2[x, zh]

    for n, (dx, dy, dz) in enumerate(offsets(NX, NY, NZ)):
        pltpu.make_async_remote_copy(
            src_ref=out2.at[x_at[dx], zh_at[dz]], dst_ref=a3.at[n + 1], send_sem=a_sem.at[8], recv_sem=a_sem.at[9],
            device_id=dev(dx, dy, dz), device_id_type=MESH).start()
    rest = a3.at[pl.ds(1, 127)]
    done3 = pltpu.make_async_remote_copy(
        src_ref=rest, dst_ref=rest, send_sem=a_sem.at[8], recv_sem=a_sem.at[9],
        device_id=partner, device_id_type=MESH)
    all_sent()
    for done in (plane_t, plane_r, column_t, column_r):
        done.wait_send()
    done3.wait_recv()
    sums = jnp.sum(a3[...], axis=0)
    shift = (NH - zh) % NH * ROWS
    own_top = [pltpu.roll(fin[n, 0, pl.ds(x, 1), :], shift, 1)[:, :ROWS] for n in range(2)]
    own_total = [pltpu.roll(fin[n, 1, pl.ds(x, 1), :], shift, 1)[:, :ROWS] for n in range(2)]
    pick_r = pltpu.roll(sums, 2 * ROWS, 1)[:, :ROWS]
    pick_t = pltpu.roll(sums, ROWS, 1)[:, :ROWS]
    squares = pltpu.roll(sums, 3 * ROWS, 1)[:, :ROWS]
    log_ratio = pick_t - own_top[1] - jnp.log(own_total[1]) - (pick_r - own_top[0] - jnp.log(own_total[0]))
    out[0:1, :] = sums[:, :ROWS]
    out[1:2, :] = jnp.sqrt(squares + 1e-06)
    out[2:3, :] = jnp.minimum(jnp.exp(log_ratio), 2.0)
    done3.wait_send()


def per_device(rollout_hidden, trainer_hidden, head_weight, token_ids, response_mask, trainer_slot):
    dma, reg = pltpu.SemaphoreType.DMA, pl.BlockSpec(memory_space=pl.ANY)
    vmem = pl.BlockSpec(memory_space=pltpu.VMEM)
    sums = pl.pallas_call(
        kernel,
        out_shape=jax.ShapeDtypeStruct((3, ROWS), F32),
        in_specs=[reg] * 5,
        out_specs=vmem,
        scratch_shapes=[
            pltpu.VMEM((2 * COLS, D), BF16),
            pltpu.VMEM((NX, NH, 4, ROWS, PART), BF16),
            pltpu.VMEM((8, 2, NX, 2, NH, HALF, FEAT), BF16),
            pltpu.VMEM((1, ROWS), jnp.int32),
            pltpu.VMEM((1, ROWS), jnp.int32),
            pltpu.VMEM((2, 128), jnp.int32),
            pltpu.VMEM((2, NX, NH, 2, 128), jnp.int32),
            pltpu.VMEM((TOK, 2 * TOK), BF16),
            pltpu.VMEM((TOK, FEAT), BF16),
            pltpu.VMEM((TOK, WIDE), F32),
            pltpu.VMEM((TOK, WIDE), F32),
            pltpu.VMEM((TOK, WIDE), F32),
            pltpu.VMEM((TOK, WIDE), F32),
            pltpu.VMEM((NX, 8, 128), F32),
            pltpu.VMEM((NX, 8, 128), F32),
            pltpu.VMEM((2, 16, 2, NX, 128), F32),
            pltpu.VMEM((2, 8, 2, NX, 128), F32),
            pltpu.VMEM((2, 2, NX, 128), F32),
            pltpu.VMEM((NX, NH, 1, 128), F32),
            pltpu.VMEM((128, 1, 128), F32),
            dma((11,)), dma((ARRIVALS,)), dma((8,)), dma((10,)),
        ],
        compiler_params=pltpu.CompilerParams(
            collective_id=0, has_side_effects=True, vmem_limit_bytes=60 * 1024 * 1024),
        cost_estimate=pl.CostEstimate(
            flops=2 * 2 * TOK * D * 2 * COLS + 2 * TOK * 2 * TOK * D, bytes_accessed=D * COLS * 2, transcendentals=2 * TOK * 2 * COLS),
    )(rollout_hidden.reshape(2, HALF, FEAT), trainer_hidden, head_weight.T,
      trainer_slot.reshape(1, ROWS), token_ids.reshape(1, ROWS))
    mask = response_mask.astype(F32)
    return tuple(sums[n] * mask for n in range(3))


def solution(mesh):
    placed = (
        P("seq", "vocab"),
        P("seq", None),
        P(None, ("seq", "vocab")),
        P("seq"),
        P("seq"),
        P("seq"),
    )
    return jax.shard_map(
        per_device,
        mesh=mesh,
        in_specs=placed,
        out_specs=(P("seq"), P("seq"), P("seq")),
        check_vma=False,
    )
```

```python
import jax
import jax.numpy as jnp
from jax import lax
from jax.experimental import pallas as pl
from jax.experimental.pallas import tpu as pltpu
from jax.sharding import PartitionSpec as P

MESH = pl.DeviceIdType.MESH
BF16 = jnp.bfloat16
F32 = jnp.float32
NX, NY, NZ, NH = 4, 4, 8, 4
ROWS = 32
HALF = 16
D = 4096
FEAT = 512
COLS = 592
WIDE = 1280
TOK = 512
GROUP = 128
PART = 1024
ARRIVALS = 86

ORDER = (
    ("fx", 0), ("start", 0), ("fx", 1), ("tzown", 0), ("fx", 3), ("tzown", 2),
    ("tl", 0), ("tr", 0), ("tzown", 1), ("sx", 0), ("yz", 0), ("head", 0),
    ("yz", 1), ("sx", 1), ("sz", 0), ("tzown", 3), ("sx", 2), ("sz", 1),
    ("near0", 0), ("tl", 1), ("tr", 1), ("spread", 0), ("yz", 2), ("near0", 2),
    ("meta1", 0), ("fx", 4), ("own1", 0), ("near0", 1), ("sz", 2), ("own1", 2),
    ("y2l", 0), ("y2r", 0), ("s2r", 0), ("s2l", 0), ("fx", 5), ("y2r", 1),
    ("near0", 3), ("y2l", 1), ("away0", 0), ("relayu", 0), ("relayd", 0), ("s2r", 1),
    ("s2l", 1), ("fx", 6), ("own1", 3), ("cross", 0), ("meta2", 0), ("near1", 0),
    ("fx", 9), ("own1", 1), ("onehot", 0), ("near1", 2), ("s2r", 2), ("s2l", 2),
    ("spread", 2), ("y2r", 2), ("fx", 7), ("s3", 0), ("near0", 4), ("away0", 1),
    ("y2l", 2), ("fx", 11), ("s3", 1), ("near1", 3), ("away1", 0), ("fx", 12),
    ("near1", 1), ("swap", 0), ("s3", 2), ("fx", 10), ("relayu", 2), ("relayd", 2),
    ("spread", 1), ("cross", 2), ("fx", 2), ("R", 0), ("swap", 2), ("relayu", 1),
    ("relayd", 1), ("fx", 13), ("spread", 3), ("near1", 4), ("swap", 3), ("T", 3),
    ("relayu", 3), ("near0", 5), ("relayd", 3), ("away1", 1), ("fx", 14), ("fx", 8),
    ("R", 2), ("far", 2), ("cross", 1), ("swap", 1), ("R", 3), ("far", 0),
    ("cross", 3), ("far", 1), ("T", 0), ("near1", 5), ("fx", 15), ("swap", 4),
    ("T", 2), ("far", 3), ("R", 1), ("R", 4), ("swap", 5), ("swap", 6),
    ("T", 1), ("TS", 0), ("swap", 7), ("R", 5), ("R", 6), ("R", 7),
    ("RS", 0),
)


def kernel(roll_in, train_in, head_in, slot_in, ids_in, out,
           w, t, r, slot_v, ids_v, line, meta, onehot, perm, lt, lr, et, er, stat_r, stat_t, a1, a2, fin, out2, a3,
           ssem, rsem, in_sem, a_sem):
    s, v = lax.axis_index("seq"), lax.axis_index("vocab")
    x, zh, c = lax.div(s, 8), lax.rem(lax.div(s, 2), 4), lax.rem(s, 2)
    zl, y = lax.div(v, 4), lax.rem(v, 4)
    z = zh * 2 + zl

    x_at = [lax.rem(x + d, NX) for d in range(NX)]
    y_at = [lax.rem(y + d, NY) for d in range(NY)]
    z_at = [lax.rem(z + d, NZ) for d in range(NZ)]
    zh_at = [lax.div(zz, 2) for zz in z_at]
    seq_x = [8 * xx + c for xx in x_at]
    seq_z = [2 * zz for zz in zh_at]
    vocab_z = [4 * lax.rem(zz, 2) for zz in z_at]

    def dev(dx=0, dy=0, dz=0):
        return (seq_x[dx % NX] + seq_z[dz % NZ], vocab_z[dz % NZ] + y_at[dy % NY])

    def offsets(xs, ys, zs):
        every = [(dx, dy, dz) for dx in range(xs) for dy in range(ys) for dz in range(zs)][1:]
        return sorted(every, key=lambda o: -min(o[0], NX - o[0]) - min(o[1], NY - o[1]) - min(o[2], NZ - o[2]))

    partner = (s + 1 - 2 * c, v)
    xm, xp, xo = x_at[3], x_at[1], x_at[2]
    xg = (x, xm, xp, xo)
    zm, zp, zo = zh_at[6], zh_at[2], zh_at[4]

    barrier = pltpu.get_barrier_semaphore()
    near = [dev(dz=d) for d in (4, 2, -2)] + [dev(dx=2)] + [dev(dx=d) for d in (1, -1)]
    near += [dev(dy=d) for d in (1, -1)] + [dev(dz=d) for d in (1, -1)] + [partner]
    for to in near:
        pl.semaphore_signal(barrier, inc=1, device_id=to, device_id_type=MESH)

    copies = [
        pltpu.make_async_copy(slot_in, slot_v, in_sem.at[6]),
        pltpu.make_async_copy(ids_in, ids_v, in_sem.at[7]),
        pltpu.make_async_copy(roll_in, r.at[v, c, x, :, zh], in_sem.at[0]),
    ]
    for q in range(4):
        copies.append(pltpu.make_async_copy(train_in.at[:, q * PART:(q + 1) * PART], t.at[x, zh, q], in_sem.at[1 + q]))
    copies.append(pltpu.make_async_copy(head_in, w.at[:COLS], in_sem.at[5]))
    for cp in copies:
        cp.start()
    for cp in copies[:2]:
        cp.wait()
    lanes = lax.broadcasted_iota(jnp.int32, (1, 128), 1)
    line[0:1, :ROWS] = slot_v[...]
    line[1:2, :ROWS] = ids_v[...]
    slots, ids = line[0:1, :], line[1:2, :]
    low = jnp.where(lanes // HALF == zh, pltpu.roll(slots, zh * HALF, 1), 0)
    high = jnp.where(lanes // HALF == NH + zh, pltpu.roll(slots, (NH - 1 + zh) * HALF, 1), 0)
    meta[c, x, zh, 0:1, :] = low + high
    meta[c, x, zh, 1:2, :] = jnp.where(lanes // ROWS == zh, pltpu.roll(ids, zh * ROWS, 1), 0)
    edge = pl.ds(WIDE - 128, 128)
    lt[:, edge] = jnp.full((TOK, 128), -jnp.inf, F32)
    lr[:, edge] = jnp.full((TOK, 128), -jnp.inf, F32)
    for cp in copies[2:7]:
        cp.wait()
    pl.semaphore_wait(barrier, len(near))

    right, left = dev(dz=1), dev(dz=-1)
    outward = tuple(zl * a + (1 - zl) * b for a, b in zip(right, left))
    inward = tuple(zl * b + (1 - zl) * a for a, b in zip(right, left))
    xr, xl = dev(dx=1), dev(dx=-1)
    yu, yd = dev(dy=1), dev(dy=-1)
    z_near, z_away = (1 - zl) * zm + zl * zp, (1 - zl) * zp + zl * zm
    zz = (zm, zp, zo)

    v_z = (1 - zl) * 4 + y
    v_up, v_dn, v_far = [zl * 4 + y_at[d] for d in (1, 3, 2)]
    w_up, w_dn, w_far = [(1 - zl) * 4 + y_at[d] for d in (1, 3, 2)]
    features = (v, v_z, v_dn, v_up, v_far, w_dn, w_up, w_far)

    block = {}

    def small(vv, xx, zq):
        return r.at[vv, c, xx, :, zq]

    for k in range(3):
        block["sz", k] = small(v, x, zz[k])
        block["sx", k] = small(v, (xm, xp, xo)[k], zh)
        block["mz", k] = meta.at[c, x, zz[k]]
        block["mx", k] = meta.at[c, (xm, xp, xo)[k]]
        block["s2l", k] = small(v, xm, zz[k])
        block["s2r", k] = small(v, xp, zz[k])
        block["s3l", k] = r.at[v, c, xo, 0, zz[k]]
        block["s3r", k] = r.at[v, c, xo, 1, zz[k]]
    block["ms", 0] = meta.at[1 - c]
    block["w", 0] = w.at[COLS:]
    order = [(x, zh)] + [(x, q) for q in zz] + [(xx, zh) for xx in xg[1:]] + [(xx, q) for xx in xg[1:] for q in zz]
    for k, (xx, zq) in enumerate(order):
        block["yu", k] = small(v_dn, xx, zq)
        block["yd", k] = small(v_up, xx, zq)
    for g in range(4):
        block["rr", g] = r.at[v_z, c, xg[g], 0]
        block["rl", g] = r.at[v_z, c, xg[g], 1]
        block["cu", g] = r.at[w_dn, c, xg[g]]
        block["cd", g] = r.at[w_up, c, xg[g]]
        block["fu", g] = r.at[v_far, c, xg[g], 1]
        block["fd", g] = r.at[v_far, c, xg[g], 0]
        block["lr", g] = r.at[w_far, c, xg[g], 0]
        block["ll", g] = r.at[w_far, c, xg[g], 1]
    for k in range(8):
        block["v", k] = r.at[features[k], 1 - c]

    def qn(k):
        return zl * (3 - k) + (1 - zl) * k

    def qf(k):
        return zl * k + (1 - zl) * (3 - k)

    def near_block(xx, k):
        return t.at[xx, z_near if k < 4 else zo, qn(k % 4)]

    def away_block(xx, k):
        return t.at[xx, z_away if k < 4 else zo, qf(k % 4)]

    quarter = {}
    for k in range(6):
        for g, xx in enumerate((x, xo)):
            block["tn%d" % g, k] = near_block(xx, k)
            block["tf%d" % g, k] = away_block(xx, k)
            quarter["tn%d" % g, k] = 3 - k % 4
            quarter["tf%d" % g, k] = k % 4
        for name, xx in (("tl", xm), ("tr", xp)):
            block[name, 4 + 2 * k] = near_block(xx, k)
            block[name, 5 + 2 * k] = away_block(xx, k)
            quarter[name, 4 + 2 * k] = 3 - k % 4
            quarter[name, 5 + 2 * k] = k % 4
    for k in range(4):
        block["tl", k] = t.at[xm, zh, qf(k)]
        block["tr", k] = t.at[xp, zh, qf((k + 2) % 4)]
        quarter["tl", k] = k
        quarter["tr", k] = (k + 2) % 4
    for k in range(2):
        block["ul", k] = t.at[xo, zh, qf(k)]
        block["ur", k] = t.at[xo, zh, qf(k + 2)]
        quarter["ul", k] = k
        quarter["ur", k] = k + 2
    def wait_key(name, k):
        if name in ("yu", "yd"):
            g = [n for n in range(4) if k in members[n]][0]
            return (name, g), r.at[v_dn if name == "yu" else v_up, c, xg[g]]
        if name in ("rr", "rl"):
            return ("rr", k), r.at[v_z, c, xg[k]]
        if name in ("fu", "fd"):
            return ("fu", k), r.at[v_far, c, xg[k]]
        if name in ("s3l", "s3r"):
            return ("s3l", k), small(v, xo, zz[k])
        if name in ("cu", "cd"):
            return (name, 0), r.at[w_dn if name == "cu" else w_up, c]
        if name in ("lr", "ll"):
            return ("lr", 0), r.at[w_far, c]
        if name == "mz":
            return (name, 0), meta.at[c, x, pl.ds(0, 3)]
        if name == "mx":
            return (name, 0), meta.at[c, pl.ds(0, 3)]
        if name in ("tl", "tr") and k >= 4:
            return ("tq", quarter[name, k]), t.at[0, pl.ds(0, 3), pl.ds(0, 2)]
        return (name, k), block[name, k]

    members = ((0, 1, 2, 3), (4, 7, 8, 9), (5, 10, 11, 12), (6, 13, 14, 15))
    wait_of = {name: wait_key(*name) for name in block}
    keys = {}
    for key, _ in wait_of.values():
        keys.setdefault(key, len(keys))
    assert len(keys) == ARRIVALS, len(keys)

    sent = {n: 0 for n in range(11)}
    waited = set()

    def send_sem(name):
        if name in ("v", "w"):
            n = 0 if name == "v" else 1
        elif name in ("rr", "rl", "cu", "cd", "fu", "fd", "lr", "ll"):
            n = 4
        elif name in ("s3l", "s3r"):
            n = 7
        elif name in ("mz", "mx", "ms"):
            n = 8 + ("mz", "mx", "ms").index(name)
        elif name in ("sz", "sx", "s2l", "s2r", "yu", "yd"):
            n = 5 if sent[5] < 32 else 6
        else:
            n = 2 if sent[2] < 48 else 3
        sent[n] += 1
        return n

    def put(name, n, ref, to, dst=None):
        pltpu.make_async_remote_copy(
            src_ref=ref, dst_ref=ref if dst is None else dst, send_sem=ssem.at[send_sem(name)],
            recv_sem=rsem.at[keys[wait_of[name, n][0]]], device_id=to, device_id_type=MESH).start()

    def all_sent():
        whole_sends = (
            r.at[:, 0], w.at[:COLS], t.at[pl.ds(0, 3)], t.at[0, pl.ds(0, 3)], r.at[pl.ds(0, 5), 0],
            r.at[:, 0, :, :, 0], r.at[pl.ds(0, 3), 0, :, :, 0], r.at[pl.ds(0, 3), 0, 0, :, 0],
            meta.at[0, 0, pl.ds(0, 3)], meta.at[0, pl.ds(0, 3)], meta.at[0],
        )
        assert tuple(sent.values()) == (8, 1, 48, 12, 32, 32, 12, 6, 3, 3, 1), sent
        for n, ref in enumerate(whole_sends):
            pltpu.make_async_remote_copy(
                src_ref=ref, dst_ref=ref, send_sem=ssem.at[n], recv_sem=ssem.at[n],
                device_id=partner, device_id_type=MESH).wait_send()

    def need(*names):
        for name in names:
            key, ref = wait_of[name]
            if key not in waited:
                waited.add(key)
                sem = rsem.at[keys[key]]
                pltpu.make_async_remote_copy(
                    src_ref=ref, dst_ref=ref, send_sem=sem, recv_sem=sem,
                    device_id=partner, device_id_type=MESH).wait_recv()

    def up_down(k, ref):
        put("yu", k, ref, yu)
        put("yd", k, ref, yd)

    own = small(v, x, zh)
    of_group = (
        [("sz", k) for k in range(3)],
        [("sx", 0)] + [("s2l", k) for k in range(3)],
        [("sx", 1)] + [("s2r", k) for k in range(3)],
        [("sx", 2)] + [(a, k) for a in ("s3l", "s3r") for k in range(3)],
    )
    whole = (
        sum(of_group, []),
        [(a, g) for a in ("rr", "rl") for g in range(4)],
        [("yu", k) for k in range(16)],
        [("yd", k) for k in range(16)],
        [(a, g) for a in ("fu", "fd") for g in range(4)],
        [("cu", g) for g in range(4)],
        [("cd", g) for g in range(4)],
        [(a, g) for a in ("lr", "ll") for g in range(4)],
    )

    def do(task, k):
        if task == "start":
            for n, d in enumerate((2, -2, 4)):
                put("sz", n, own, dev(dz=d))
            for n, d in enumerate((1, -1, 2)):
                put("sx", n, own, dev(dx=d))
            up_down(0, own)
            for n, d in enumerate((2, -2, 4)):
                put("mz", n, meta.at[c, x, zh], dev(dz=d))
        elif task == "head":
            copies[7].wait()
            put("w", 0, w.at[:COLS], partner, w.at[COLS:])
        elif task == "fx" and k < 4:
            put("tl", k, t.at[x, zh, qf(k)], xr)
            put("tr", k, t.at[x, zh, qf((k + 2) % 4)], xl)
        elif task == "fx":
            name = ("tf0", (k - 5) // 2) if k % 2 else ("tn0", (k - 4) // 2)
            need(name)
            put("tl", k, block[name], xr)
            put("tr", k, block[name], xl)
        elif task == "tzown":
            put("tn0", k, t.at[x, zh, qf(k)], outward)
        elif task == "meta1":
            need(("mz", 0), ("mz", 1), ("mz", 2))
            for n, d in enumerate((1, -1, 2)):
                put("mx", n, meta.at[c, x], dev(dx=d))
        elif task == "meta2":
            need(("mx", 0), ("mx", 1), ("mx", 2))
            put("ms", 0, meta.at[c], partner)
        elif task == "sz":
            need(("sz", k))
            ref = block["sz", k]
            put("s2l", k, ref, xr)
            put("s2r", k, ref, xl)
        elif task == "yz":
            need(("sz", k))
            up_down(1 + k, block["sz", k])
        elif task == "sx":
            need(("sx", k))
            up_down(4 + k, block["sx", k])
        elif task == "s2l":
            need(("s2l", k))
            put("s3l", k, r.at[v, c, xm, 0, zz[k]], xr)
        elif task == "y2l":
            need(("s2l", k))
            up_down(7 + k, block["s2l", k])
        elif task == "s2r":
            need(("s2r", k))
            put("s3r", k, r.at[v, c, xp, 1, zz[k]], xl)
        elif task == "y2r":
            need(("s2r", k))
            up_down(10 + k, block["s2r", k])
        elif task == "s3":
            need(("s3l", k), ("s3r", k))
            up_down(13 + k, small(v, xo, zz[k]))
        elif task == "spread":
            need(*of_group[k])
            put("rr", k, r.at[v, c, xg[k], 0], right)
            put("rl", k, r.at[v, c, xg[k], 1], left)
        elif task == "cross":
            need(("rr", k), ("rl", k))
            put("cu", k, r.at[v_z, c, xg[k]], yu)
            put("cd", k, r.at[v_z, c, xg[k]], yd)
        elif task == "relayu":
            need(*[("yu", i) for i in members[k]])
            put("fu", k, r.at[v_dn, c, xg[k], 1], yu)
        elif task == "relayd":
            need(*[("yd", i) for i in members[k]])
            put("fd", k, r.at[v_up, c, xg[k], 0], yd)
        elif task == "far":
            need(("fu", k), ("fd", k))
            put("lr", k, r.at[v_far, c, xg[k], 0], right)
            put("ll", k, r.at[v_far, c, xg[k], 1], left)
        elif task == "swap":
            need(*whole[k])
            put("v", k, r.at[features[k], c], partner)
        elif task in ("near0", "near1"):
            g = task[-1]
            need(("tn" + g, k))
            ref = block["tn" + g, k]
            put("tf" + g, k, ref, inward)
        elif task in ("away0", "away1"):
            g = task[-1]
            need(("tf" + g, k))
            put("tn" + g, 4 + k, block["tf" + g, k], outward)
        elif task == "tl":
            need(("tl", k))
            put("ul", k, block["tl", k], xr)
        elif task == "tr":
            need(("tr", k))
            put("ur", k, block["tr", k], xl)
        elif task == "own1":
            name = ("ul", k) if k < 2 else ("ur", k - 2)
            need(name)
            put("tn1", k, block[name], outward)
        elif task == "R":
            need(("v", k), ("w", 0), *whole[k])
            rollout_part(features[k])
        elif task == "T":
            need(("w", 0), *[name for name, q in quarter.items() if q == k])
            trainer_part(qf(k))
        elif task == "onehot":
            need(("ms", 0))
            fill_onehot()
        elif task == "TS":
            for xx in range(NX):
                train_stats(xx, 0)
        elif task == "RS":
            for xx in range(NX):
                roll_stats(xx, 0)

    def fill_onehot():
        place = lax.broadcasted_iota(jnp.int32, (TOK, GROUP), 0)
        for cc in range(2):
            for xx in range(NX):
                slot = meta[cc, xx, 0, 0:1, :]
                for zq in range(1, NH):
                    slot = slot + meta[cc, xx, zq, 0:1, :]
                token = (slot >> 6) * ROWS + (slot & (ROWS - 1))
                token = jnp.where(((slot >> 5) & 1) == c, token, -1)
                n = cc * NX + xx
                onehot[:, n * GROUP:(n + 1) * GROUP] = jnp.where(place == token, 1.0, 0.0).astype(BF16)

    def logits(rows, f):
        return lax.dot_general(rows, w[:, f], (((1,), (1,)), ((), ())), preferred_element_type=F32)

    begun = set()

    def add(logit, part):
        if id(logit) in begun:
            logit[:, :2 * COLS] += part
        else:
            begun.add(id(logit))
            logit[:, :2 * COLS] = part

    def rollout_part(vv):
        rows = r[vv].reshape(2 * TOK, FEAT)
        perm[...] = jnp.dot(onehot[...], rows, preferred_element_type=F32).astype(BF16)
        add(lr, logits(perm[...], pl.ds(pl.multiple_of(vv * FEAT, FEAT), FEAT)))

    def trainer_part(q):
        rows = t[:, :, pl.ds(q, 1)].reshape(TOK, PART)
        add(lt, logits(rows, pl.ds(pl.multiple_of(q * PART, PART), PART)))

    lane = lax.broadcasted_iota(jnp.int32, (GROUP, 128), 1)
    diagonal = lax.broadcasted_iota(jnp.int32, (GROUP, 128), 0) == lane

    def to_row(values):
        return jnp.sum(jnp.where(diagonal, values, 0), axis=0, keepdims=True)

    def to_column(values):
        return jnp.sum(jnp.where(diagonal, values, 0), axis=1, keepdims=True)

    def rows_of(xx):
        if isinstance(xx, int):
            return pl.ds(xx * GROUP, GROUP)
        return pl.ds(pl.multiple_of(xx * GROUP, GROUP), GROUP)

    tiles = [pl.ds(128 * j, 128) for j in range(WIDE // 128)]

    def group_stats(logit, ex, stat, xx):
        rows = rows_of(xx)
        top = logit[rows, tiles[0]]
        for tile in tiles[1:]:
            top = jnp.maximum(top, logit[rows, tile])
        top = jnp.max(top, axis=1, keepdims=True)
        total = jnp.zeros((GROUP, 128), F32)
        for tile in tiles:
            e = jnp.exp(logit[rows, tile] - top)
            ex[rows, tile] = e
            total = total + e
        stat[xx, 0:1, :] = to_row(top)
        stat[xx, 1:2, :] = to_row(jnp.sum(total, axis=1, keepdims=True))

    def group_picks(logit, stat, xx):
        rows = rows_of(xx)
        ids = meta[c, xx, 0, 1:2, :]
        for zq in range(1, NH):
            ids = ids + meta[c, xx, zq, 1:2, :]
        ids = to_column(ids)
        pick = jnp.zeros((GROUP, 128), F32)
        for n, tile in enumerate(tiles):
            column = lanes + 128 * n
            column = jnp.where(
                column < COLS, column + (s * 8 + v) * COLS,
                jnp.where(column < 2 * COLS, column + ((s + 1 - 2 * c) * 8 + v) * COLS - COLS, -1))
            pick = pick + jnp.where(column == ids, logit[rows, tile], 0.0)
        stat[xx, 2:3, :] = to_row(jnp.sum(pick, axis=1, keepdims=True))

    def train_stats(xx, carry):
        group_stats(lt, et, stat_t, xx)
        group_picks(lt, stat_t, xx)
        return carry

    def roll_stats(xx, carry):
        group_stats(lr, er, stat_r, xx)
        return carry

    def roll_picks(xx, carry):
        group_picks(lr, stat_r, xx)
        return carry

    def exchange(buf, sem, away):
        count = len(away) + 1
        for n, offset in enumerate(away):
            pltpu.make_async_remote_copy(
                src_ref=buf.at[0], dst_ref=buf.at[n + 1], send_sem=a_sem.at[sem], recv_sem=a_sem.at[sem + 1],
                device_id=dev(*offset), device_id_type=MESH).start()
        rest = buf.at[pl.ds(1, count - 1)]
        return pltpu.make_async_remote_copy(
            src_ref=rest, dst_ref=rest, send_sem=a_sem.at[sem], recv_sem=a_sem.at[sem + 1],
            device_id=partner, device_id_type=MESH)

    def merge(buf, count):
        top = buf[0, 0]
        for d in range(1, count):
            top = jnp.maximum(top, buf[d, 0])
        total = jnp.zeros_like(top)
        for d in range(count):
            total = total + buf[d, 1] * jnp.exp(buf[d, 0] - top)
        return top, total

    def plane(n, stat):
        a1[n, 0, 0] = stat[:, 0, :]
        a1[n, 0, 1] = stat[:, 1, :]
        return exchange(a1.at[n], 4 * n, offsets(NX, NY, 1))

    def column_z(n, before):
        before.wait_recv()
        top, total = merge(a1.at[n], 16)
        a2[n, 0, 0] = top
        a2[n, 0, 1] = total
        return exchange(a2.at[n], 4 * n + 2, offsets(1, 1, NZ))

    def finish(n, before):
        before.wait_recv()
        top, total = merge(a2.at[n], 8)
        fin[n, 0] = top
        fin[n, 1] = total

    for task, k in ORDER:
        do(task, k)
        if task == "TS":
            plane_t = plane(1, stat_t)
    plane_r = plane(0, stat_r)
    column_t = column_z(1, plane_t)
    lax.fori_loop(0, NX, roll_picks, 0)
    column_r = column_z(0, plane_r)
    finish(1, column_t)
    for xx in range(NX):
        scale_t = to_column(jnp.exp(stat_t[xx, 0:1, :] - fin[1, 0, xx:xx + 1, :]) / fin[1, 1, xx:xx + 1, :])
        for tile in tiles:
            et[rows_of(xx), tile] = et[rows_of(xx), tile] * scale_t
    finish(0, column_r)

    def compare(xx, carry):
        rows = rows_of(xx)
        scale_r = jnp.exp(stat_r[xx, 0:1, :] - fin[0, 0, pl.ds(xx, 1), :]) / fin[0, 1, pl.ds(xx, 1), :]
        scale_r = to_column(scale_r)
        shared = jnp.zeros((GROUP, 128), F32)
        squares = jnp.zeros((GROUP, 128), F32)
        for tile in tiles:
            p = er[rows, tile] * scale_r
            q = et[rows, tile]
            shared = shared + jnp.minimum(p, q)
            squares = squares + (q - p) * (q - p)
        shared = to_row(jnp.sum(shared, axis=1, keepdims=True))
        squares = to_row(jnp.sum(squares, axis=1, keepdims=True))
        values = (shared, squares, stat_r[xx, 2:3, :], stat_t[xx, 2:3, :])
        part = lax.broadcasted_iota(jnp.int32, (1, 128), 1) // ROWS
        for zq in range(NH):
            one = jnp.zeros((1, 128), F32)
            for k in range(4):
                one = one + jnp.where(part == k, pltpu.roll(values[k], ((k - zq) % 4) * ROWS, 1), 0.0)
            out2[xx, zq] = one
        return carry
    for xx in range(NX):
        compare(xx, 0)

    a3[0] = out2[x, zh]

    for n, (dx, dy, dz) in enumerate(offsets(NX, NY, NZ)):
        pltpu.make_async_remote_copy(
            src_ref=out2.at[x_at[dx], zh_at[dz]], dst_ref=a3.at[n + 1], send_sem=a_sem.at[8], recv_sem=a_sem.at[9],
            device_id=dev(dx, dy, dz), device_id_type=MESH).start()
    rest = a3.at[pl.ds(1, 127)]
    done3 = pltpu.make_async_remote_copy(
        src_ref=rest, dst_ref=rest, send_sem=a_sem.at[8], recv_sem=a_sem.at[9],
        device_id=partner, device_id_type=MESH)
    all_sent()
    for done in (plane_t, plane_r, column_t, column_r):
        done.wait_send()
    done3.wait_recv()
    sums = jnp.sum(a3[...], axis=0)
    shift = (NH - zh) % NH * ROWS
    own_top = [pltpu.roll(fin[n, 0, pl.ds(x, 1), :], shift, 1)[:, :ROWS] for n in range(2)]
    own_total = [pltpu.roll(fin[n, 1, pl.ds(x, 1), :], shift, 1)[:, :ROWS] for n in range(2)]
    pick_r = pltpu.roll(sums, 2 * ROWS, 1)[:, :ROWS]
    pick_t = pltpu.roll(sums, ROWS, 1)[:, :ROWS]
    squares = pltpu.roll(sums, 3 * ROWS, 1)[:, :ROWS]
    log_ratio = pick_t - own_top[1] - jnp.log(own_total[1]) - (pick_r - own_top[0] - jnp.log(own_total[0]))
    out[0:1, :] = sums[:, :ROWS]
    out[1:2, :] = jnp.sqrt(squares + 1e-06)
    out[2:3, :] = jnp.minimum(jnp.exp(log_ratio), 2.0)
    done3.wait_send()


def per_device(rollout_hidden, trainer_hidden, head_weight, token_ids, response_mask, trainer_slot):
    dma, reg = pltpu.SemaphoreType.DMA, pl.BlockSpec(memory_space=pl.ANY)
    vmem = pl.BlockSpec(memory_space=pltpu.VMEM)
    sums = pl.pallas_call(
        kernel,
        out_shape=jax.ShapeDtypeStruct((3, ROWS), F32),
        in_specs=[reg] * 5,
        out_specs=vmem,
        scratch_shapes=[
            pltpu.VMEM((2 * COLS, D), BF16),
            pltpu.VMEM((NX, NH, 4, ROWS, PART), BF16),
            pltpu.VMEM((8, 2, NX, 2, NH, HALF, FEAT), BF16),
            pltpu.VMEM((1, ROWS), jnp.int32),
            pltpu.VMEM((1, ROWS), jnp.int32),
            pltpu.VMEM((2, 128), jnp.int32),
            pltpu.VMEM((2, NX, NH, 2, 128), jnp.int32),
            pltpu.VMEM((TOK, 2 * TOK), BF16),
            pltpu.VMEM((TOK, FEAT), BF16),
            pltpu.VMEM((TOK, WIDE), F32),
            pltpu.VMEM((TOK, WIDE), F32),
            pltpu.VMEM((TOK, WIDE), F32),
            pltpu.VMEM((TOK, WIDE), F32),
            pltpu.VMEM((NX, 8, 128), F32),
            pltpu.VMEM((NX, 8, 128), F32),
            pltpu.VMEM((2, 16, 2, NX, 128), F32),
            pltpu.VMEM((2, 8, 2, NX, 128), F32),
            pltpu.VMEM((2, 2, NX, 128), F32),
            pltpu.VMEM((NX, NH, 1, 128), F32),
            pltpu.VMEM((128, 1, 128), F32),
            dma((11,)), dma((ARRIVALS,)), dma((8,)), dma((10,)),
        ],
        compiler_params=pltpu.CompilerParams(
            collective_id=0, has_side_effects=True, vmem_limit_bytes=60 * 1024 * 1024),
        cost_estimate=pl.CostEstimate(
            flops=2 * 2 * TOK * D * 2 * COLS + 2 * TOK * 2 * TOK * D, bytes_accessed=D * COLS * 2, transcendentals=2 * TOK * 2 * COLS),
    )(rollout_hidden.reshape(2, HALF, FEAT), trainer_hidden, head_weight.T,
      trainer_slot.reshape(1, ROWS), token_ids.reshape(1, ROWS))
    mask = response_mask.astype(F32)
    return tuple(sums[n] * mask for n in range(3))


def solution(mesh):
    placed = (
        P("seq", "vocab"),
        P("seq", None),
        P(None, ("seq", "vocab")),
        P("seq"),
        P("seq"),
        P("seq"),
    )
    return jax.shard_map(
        per_device,
        mesh=mesh,
        in_specs=placed,
        out_specs=(P("seq"), P("seq"), P("seq")),
        check_vma=False,
    )
```
